32 devices in a mesh: batch: 16 (over z, y, core), span: 2 (over x).
Axes of the slice: x: 2, y: 2, z: 4, core: 2. Of those that a mesh axis runs over, the one named last changes fastest.
Arguments:
- image_tokens: bfloat16 [32, 256, 512], P('batch'), may hold values from -400 to 400
- captions: bfloat16 [256, 512], P(('batch', 'span')), may hold values from -6 to 6
- owner: int32 [256], P(('batch', 'span')), may hold values from 0 to 31
- w_query: bfloat16 [512, 512], replicated, may hold values from -0.25 to 0.25
- w_key: bfloat16 [512, 512], replicated, may hold values from -0.25 to 0.25
- w_value: bfloat16 [512, 512], replicated, may hold values from -0.25 to 0.25
- w_out: bfloat16 [512, 512], replicated, may hold values from -0.25 to 0.25
Outputs:
- caption_grad: float32 [256, 512], P(('batch', 'span'))
- token_grad: float32 [32, 256, 512], P('batch')
The draws below stay inside these ranges and needn't reach their ends.
Inputs may be any that keep to these rules, and one draw needn't show every extreme that they name: `owner`: each caption names one image.
All inputs are finite; a program needn't handle non-finite values.
Results may differ from the reference program's by a relative error of at most 0.039.
The reference program's roundings to bfloat16 on the way count: a program that leaves them out, or rounds other values in their place, can miss the bound.
Values may be sent and summed in bfloat16 or wider, within the bound.
A program may use at most 64 MiB of HBM per device.

```python
import math
import jax
import jax.numpy as jnp
from jax import lax

HEADS = 8
HEAD_DIM = 64
D = 512
PATCHES = 256
IMAGES = 32
CAPTIONS = 256


def draw_image_tokens(key, part):
    base_key = jax.random.fold_in(key, 0)
    base = jax.random.truncated_normal(base_key, -6.0, 6.0, (IMAGES, PATCHES, D), jnp.float32)
    return base.astype(jnp.bfloat16)


def with_ends(drawn, rng, low, top_value):
    index_at = [jax.random.randint(jax.random.fold_in(rng, axis), (), 0, length) for axis, length in enumerate(drawn.shape)]
    main_axis = drawn.shape.index(max(drawn.shape))
    beside = index_at[:main_axis] + [(index_at[main_axis] + 1) % drawn.shape[main_axis]] + index_at[main_axis + 1:]
    return drawn.at[tuple(index_at)].set(low).at[tuple(beside)].set(top_value)


def block_levels(stream_key, dims, pieces, low, top_value):
    def one(dim, shards_of):
        heights = jax.random.uniform(jax.random.fold_in(jax.random.fold_in(stream_key, 6), dim), (shards_of,), jnp.float32, low / len(pieces), top_value / len(pieces))
        return jnp.repeat(jnp.exp(heights), dims[dim] // shards_of).reshape((-1,) + (1,) * (len(dims) - dim - 1))

    loudness = one(*pieces[0])
    for cut in pieces[1:]:
        loudness = loudness * one(*cut)
    return loudness


def normal_values(key, dims, spread, reach, cuts=(), kind=jnp.bfloat16):
    result = spread * jax.random.normal(key, dims, jnp.float32)
    if cuts:
        result = result * block_levels(key, dims, cuts, -0.22, 0.18)
    return jnp.clip(result, -reach, reach).astype(kind)


def setup_inputs(seed: int = 0) -> dict:
    streams_of = jax.random.split(jax.random.key(seed), 8)
    image_tokens = draw_image_tokens(jax.random.fold_in(streams_of[7], 71), 0)
    captions = normal_values(streams_of[1], (CAPTIONS, D), 1.0, 6.0, ((0, 32),))
    owner = with_ends(jax.random.randint(streams_of[2], (CAPTIONS,), 0, IMAGES), jax.random.fold_in(streams_of[2], 1), 0, IMAGES - 1).astype(jnp.int32)
    w_query = normal_values(streams_of[3], (D, D), D ** -0.5, 0.25)
    w_key = normal_values(streams_of[4], (D, D), D ** -0.5, 0.25)
    w_value = normal_values(streams_of[5], (D, D), D ** -0.5, 0.25)
    w_out = normal_values(streams_of[6], (D, D), D ** -0.5, 0.25)
    return {"image_tokens": image_tokens, "captions": captions, "owner": owner, "w_query": w_query, "w_key": w_key, "w_value": w_value, "w_out": w_out}


LOGIT_SCALE = 10.0
LOGIT_BIAS = -2.0
NORM_EPS = 1e-06

def pair_loss(query, keys, values, caption_f, w_out, owner_block, image_base):
    count = query.shape[0]
    images = keys.shape[0]
    patches = keys.shape[1]
    width = keys.shape[2]
    query_heads = query.reshape(count, HEADS, HEAD_DIM)
    key_heads = keys.reshape(images, patches, HEADS, HEAD_DIM)
    value_heads = values.reshape(images, patches, HEADS, HEAD_DIM)
    scores = jnp.einsum('che,iphe->cihp', query_heads, key_heads, preferred_element_type=jnp.float32) * HEAD_DIM ** (-0.5)
    weights = jax.nn.softmax(scores, axis=-1).astype(jnp.bfloat16)
    pooled = jnp.einsum('cihp,iphe->cihe', weights, value_heads, preferred_element_type=jnp.float32)
    pooled = pooled.reshape(count * images, width).astype(jnp.bfloat16)
    mixed = jnp.dot(pooled, w_out, preferred_element_type=jnp.float32).reshape(count, images, width)
    inner = lax.optimization_barrier(jnp.sum(mixed * caption_f[:, None, :], axis=-1))
    mixed_norm = jnp.sqrt(lax.optimization_barrier(jnp.sum(mixed * mixed, axis=-1)) + NORM_EPS)
    caption_norm = jnp.sqrt(lax.optimization_barrier(jnp.sum(caption_f * caption_f, axis=-1)) + NORM_EPS)
    cosine = inner / (mixed_norm * caption_norm[:, None])
    logits = LOGIT_SCALE * cosine + LOGIT_BIAS
    image_ids = image_base + jnp.arange(images, dtype=jnp.int32)
    labels = jnp.where(owner_block[:, None] == image_ids[None, :], 1.0, -1.0).astype(jnp.float32)
    return jnp.sum(jax.nn.softplus(-labels * logits))

def block_grads(caption_block, owner_block, keys, values, w_query, w_out, image_base):
    query = jnp.dot(caption_block, w_query, preferred_element_type=jnp.float32).astype(jnp.bfloat16)
    caption_f = caption_block.astype(jnp.float32)

    def local(query_in, keys_in, values_in, caption_in):
        return pair_loss(query_in, keys_in, values_in, caption_in, w_out, owner_block, image_base)
    value, pull = jax.vjp(local, query, keys, values, caption_f)
    grad_query, grad_keys, grad_values, grad_direct = pull(jnp.ones((), jnp.float32))
    return (value, grad_query, grad_keys.astype(jnp.float32), grad_values.astype(jnp.float32), grad_direct)

def reference(image_tokens, captions, owner, w_query, w_key, w_value, w_out):
    token_rows = image_tokens.reshape(IMAGES * PATCHES, D)
    keys = jnp.dot(token_rows, w_key, preferred_element_type=jnp.float32).astype(jnp.bfloat16).reshape(IMAGES, PATCHES, D)
    values = jnp.dot(token_rows, w_value, preferred_element_type=jnp.float32).astype(jnp.bfloat16).reshape(IMAGES, PATCHES, D)
    group = math.gcd(CAPTIONS, 16)

    def step(carry, item):
        grad_keys, grad_values = carry
        caption_block, owner_block = item
        value, grad_query, more_keys, more_values, grad_direct = block_grads(caption_block, owner_block, keys, values, w_query, w_out, 0)
        caption_part = grad_direct + jnp.dot(grad_query.astype(jnp.bfloat16), w_query.T, preferred_element_type=jnp.float32)
        return ((grad_keys + more_keys, grad_values + more_values), caption_part)
    init = (jnp.zeros((IMAGES, PATCHES, D), jnp.float32), jnp.zeros((IMAGES, PATCHES, D), jnp.float32))
    items = (captions.reshape(CAPTIONS // group, group, D), owner.reshape(CAPTIONS // group, group))
    (grad_keys, grad_values), caption_parts = lax.scan(step, init, items)
    caption_grad = 16.0 * caption_parts.reshape(CAPTIONS, D)
    keys_b = grad_keys.reshape(IMAGES * PATCHES, D).astype(jnp.bfloat16)
    values_b = grad_values.reshape(IMAGES * PATCHES, D).astype(jnp.bfloat16)
    token_part = jnp.dot(keys_b, w_key.T, preferred_element_type=jnp.float32)
    token_part = token_part + jnp.dot(values_b, w_value.T, preferred_element_type=jnp.float32)
    token_grad = (PATCHES * token_part).reshape(IMAGES, PATCHES, D)
    return (caption_grad, token_grad)
```

```python
import functools
import math

import jax
import jax.numpy as jnp
from jax import lax
from jax.experimental import pallas as pl
from jax.experimental.pallas import tpu as pltpu
from jax.sharding import PartitionSpec as P

HEAD_DIM = 64
LOGIT_SCALE = 10.0
LOGIT_BIAS = -2.0
NORM_EPS = 1e-06
CAPTION_SCALE = 16.0
LANES = 128
GROUP = 256
HEADS_IN_GROUP = GROUP // HEAD_DIM
F32 = jnp.float32
BF16 = jnp.bfloat16
MESH = pl.DeviceIdType.MESH


def dot(a, b):
    return jnp.dot(a, b, preferred_element_type=F32)


def dot_t(a, b):
    return lax.dot_general(a, b, (((1,), (1,)), ((), ())), preferred_element_type=F32)


def head_stack(x):
    head = lax.broadcasted_iota(jnp.int32, x.shape, 1) // HEAD_DIM
    return jnp.concatenate(
        [jnp.where(head == h, x, jnp.zeros_like(x)) for h in range(HEADS_IN_GROUP)], axis=0
    )


def head_blocks(x, width):
    return jnp.concatenate(
        [
            x[h * HEAD_DIM : (h + 1) * HEAD_DIM, h * width : (h + 1) * width]
            for h in range(HEADS_IN_GROUP)
        ],
        axis=0,
    )


def pair_kernel(
    nb,
    ns,
    images,
    captions_ref,
    owner_ref,
    tokens_hbm,
    wq_hbm,
    wk_hbm,
    wv_hbm,
    wo_hbm,
    gk_out,
    gv_out,
    sum_out,
    tokens,
    wq,
    wk,
    wv,
    wo,
    keys,
    values,
    keys_t,
    values_t,
    prob,
    prob_b,
    gk,
    gv,
    caps,
    part,
    parts_in,
    load_sem,
    cap_send,
    cap_recv,
    span_send,
    span_recv,
    part_send,
    part_recv,
):
    me = lax.axis_index("batch")
    my_span = lax.axis_index("span")
    rows = captions_ref.shape[0]
    d = captions_ref.shape[1]
    half = d // 2
    patches = tokens.shape[0] // images
    groups = d // GROUP
    block = math.gcd(nb * rows, LANES)
    slots = block // rows
    blocks = nb * rows // block
    stacked = HEADS_IN_GROUP * block

    def peer_of(step):
        return lax.rem(me + step, nb)

    def span_of(step):
        return lax.rem(my_span + step, ns)

    barrier = pltpu.get_barrier_semaphore()

    @pl.loop(1, nb)
    def _(step):
        pl.semaphore_signal(
            barrier, inc=1, device_id={"batch": peer_of(step)}, device_id_type=MESH
        )

    for step in range(1, ns):
        pl.semaphore_signal(
            barrier, inc=1, device_id={"span": span_of(step)}, device_id_type=MESH
        )

    loads = [
        pltpu.make_async_copy(src, dst, load_sem.at[n])
        for n, (src, dst) in enumerate(
            ((tokens_hbm, tokens), (wk_hbm, wk), (wv_hbm, wv), (wq_hbm, wq), (wo_hbm, wo))
        )
    ]
    for load in loads:
        load.start()

    mine = captions_ref[...].astype(F32)
    folded = jnp.concatenate([mine[:, :half], mine[:, half:]], axis=0)
    owners = jnp.broadcast_to(owner_ref[...].astype(F32), (rows, LANES))
    owners = jnp.concatenate([owners, owners], axis=0)
    caps[0, me] = jnp.concatenate([folded, owners], axis=1).astype(BF16)

    pl.semaphore_wait(barrier, nb + ns - 2)

    def cap_copy(step, slot):
        return pltpu.make_async_remote_copy(
            src_ref=caps.at[0, me],
            dst_ref=caps.at[0, me],
            send_sem=cap_send.at[step],
            recv_sem=cap_recv.at[slot],
            device_id={"batch": peer_of(step)},
            device_id_type=MESH,
        )

    def part_copy(step, slot):
        return pltpu.make_async_remote_copy(
            src_ref=part.at[peer_of(step)],
            dst_ref=parts_in.at[me],
            send_sem=part_send.at[step],
            recv_sem=part_recv.at[slot],
            device_id={"batch": peer_of(step)},
            device_id_type=MESH,
        )

    def span_copy(step, slot):
        return pltpu.make_async_remote_copy(
            src_ref=caps.at[0],
            dst_ref=caps.at[ns - step],
            send_sem=span_send.at[step],
            recv_sem=span_recv.at[slot],
            device_id={"span": span_of(step)},
            device_id_type=MESH,
        )

    @pl.loop(1, nb)
    def _(step):
        cap_copy(step, me).start()

    for load in loads[:3]:
        load.wait()
    for i in range(images):
        at = pl.ds(i * patches, patches)
        found = dot(tokens[at, :], wk[...])
        keys[at, :] = found.astype(BF16)
        keys_t[:, at] = found.T.astype(BF16)
        found = dot(tokens[at, :], wv[...])
        values[at, :] = found.astype(BF16)
        values_t[:, at] = found.T.astype(BF16)
    gk[...] = jnp.zeros_like(gk)
    gv[...] = jnp.zeros_like(gv)
    for load in loads[3:]:
        load.wait()

    @pl.loop(1, nb)
    def _(step):
        cap_copy(step, peer_of(step)).wait_recv()

    for step in range(1, ns):
        span_copy(step, ns - step).start()

    def run_block(slot, which, own):
        held = caps[which, pl.ds(slot, slots)].astype(F32)
        caption = jnp.concatenate(
            [
                held[:, :rows, :half].reshape(block, half),
                held[:, rows:, :half].reshape(block, half),
            ],
            axis=1,
        )
        owner = held[:, :rows, half:].reshape(block, LANES)[:, :1]
        query = (dot(caption.astype(BF16), wq[...]) * HEAD_DIM**-0.5).astype(BF16)
        queries = [head_stack(query[:, g * GROUP : (g + 1) * GROUP]) for g in range(groups)]

        pooled = []
        for i in range(images):
            at = slice(i * patches, (i + 1) * patches)
            found = []
            for g in range(groups):
                cols = slice(g * GROUP, (g + 1) * GROUP)
                to = slice(g * stacked, (g + 1) * stacked)
                scores = dot_t(keys[at, cols], queries[g])
                scores = jnp.exp(scores - jnp.max(scores, axis=0, keepdims=True))
                scores = scores * (1.0 / jnp.sum(scores, axis=0, keepdims=True))
                prob[at, to] = scores
                weights = scores.astype(BF16)
                prob_b[at, to] = weights
                found.append(head_blocks(dot(values_t[cols, at], weights), block))
            pooled.append(jnp.concatenate(found, axis=0).T.astype(BF16))
        mixed = dot(jnp.concatenate(pooled, axis=0), wo[...])
        caption_2 = jnp.concatenate([caption] * images, axis=0)
        owner_2 = jnp.concatenate([owner] * images, axis=0)
        image = (
            lax.broadcasted_iota(jnp.int32, (images * block, 1), 0) // block + me * images
        ).astype(F32)
        inner = jnp.sum(mixed * caption_2, axis=1, keepdims=True)
        mixed_inv = lax.rsqrt(jnp.sum(mixed * mixed, axis=1, keepdims=True) + NORM_EPS)
        caption_inv = lax.rsqrt(jnp.sum(caption * caption, axis=1, keepdims=True) + NORM_EPS)
        caption_inv = jnp.concatenate([caption_inv] * images, axis=0)
        cosine = inner * mixed_inv * caption_inv
        logit = LOGIT_SCALE * cosine + LOGIT_BIAS
        label = jnp.where(owner_2 == image, 1.0, -1.0)
        slope = -LOGIT_SCALE * label / (1.0 + jnp.exp(label * logit))
        across = slope * mixed_inv * caption_inv
        grad_mixed = across * caption_2 - (slope * cosine * mixed_inv * mixed_inv) * mixed
        grad_pooled = dot_t(grad_mixed.astype(BF16), wo[...]).astype(BF16)
        if own:
            direct = across * mixed - (slope * cosine * caption_inv * caption_inv) * caption_2
            direct = sum(direct[i * block : (i + 1) * block] for i in range(images))

        grad_query = []
        for g in range(groups):
            cols = slice(g * GROUP, (g + 1) * GROUP)
            to = slice(g * stacked, (g + 1) * stacked)
            total = None
            for i in range(images):
                at = slice(i * patches, (i + 1) * patches)
                grads = head_stack(grad_pooled[i * block : (i + 1) * block, cols])
                grad_weights = dot_t(values[at, cols], grads)
                gv[at, cols] += dot(prob_b[at, to], grads)
                weights = prob[at, to]
                grad_scores = weights * (
                    grad_weights - jnp.sum(weights * grad_weights, axis=0, keepdims=True)
                )
                grad_scores = grad_scores.astype(BF16)
                gk[at, cols] += dot(grad_scores, queries[g])
                if own:
                    found = head_blocks(dot(keys_t[cols, at], grad_scores), block)
                    total = found if total is None else total + found
            grad_query.append(total)
        if own:
            grad_query = jnp.concatenate(grad_query, axis=0).T * HEAD_DIM**-0.5
            grad = direct + dot_t(grad_query.astype(BF16), wq[...])
            grad = grad.reshape(slots, rows, d)
            part[pl.ds(slot, slots)] = jnp.concatenate(
                [grad[:, :, :half], grad[:, :, half:]], axis=1
            ).astype(BF16)

    def run_all(which, own):
        if blocks == 1:
            run_block(0, which, own)
        else:

            @pl.loop(0, blocks)
            def _(n):
                run_block(n * slots, which, own)

    run_all(0, True)

    @pl.loop(1, nb)
    def _(step):
        part_copy(step, me).start()

    for step in range(1, ns):
        span_copy(step, step).wait_recv()
        run_all(step, False)

    gk_out[...] = gk[...].astype(BF16)
    gv_out[...] = gv[...].astype(BF16)

    @pl.loop(1, nb)
    def _(step):
        part_copy(step, peer_of(step)).wait_recv()

    parts_in[me] = part[me]
    sum_out[...] = jnp.sum(parts_in[...].astype(F32), axis=0)

    @pl.loop(1, nb)
    def _(step):
        cap_copy(step, me).wait_send()
        part_copy(step, me).wait_send()

    for step in range(1, ns):
        span_copy(step, ns - step).wait_send()


def token_kernel(patches, sum_ref, gk, gv, wk, wv, caption_out, token_out):
    rows, d = caption_out.shape
    summed = sum_ref[...] * CAPTION_SCALE
    caption_out[...] = jnp.concatenate([summed[:rows], summed[rows:]], axis=1)
    token_out[...] = patches * (dot_t(gk[...], wk[...]) + dot_t(gv[...], wv[...]))


def on_device(nb, ns, image_tokens, captions, owner, w_query, w_key, w_value, w_out):
    images, patches, d = image_tokens.shape
    rows = captions.shape[0]
    total = images * patches
    block = math.gcd(nb * rows, LANES)
    vmem = pl.BlockSpec(memory_space=pltpu.VMEM)
    anywhere = pl.BlockSpec(memory_space=pl.ANY)
    heads = d // HEAD_DIM
    dma = pltpu.SemaphoreType.DMA
    gk, gv, summed = pl.pallas_call(
        functools.partial(pair_kernel, nb, ns, images),
        out_shape=(
            jax.ShapeDtypeStruct((total, d), BF16),
            jax.ShapeDtypeStruct((total, d), BF16),
            jax.ShapeDtypeStruct((2 * rows, d // 2), F32),
        ),
        in_specs=[vmem, vmem] + [anywhere] * 5,
        out_specs=(vmem, vmem, vmem),
        scratch_shapes=[
            pltpu.VMEM((total, d), BF16),
            pltpu.VMEM((d, d), BF16),
            pltpu.VMEM((d, d), BF16),
            pltpu.VMEM((d, d), BF16),
            pltpu.VMEM((d, d), BF16),
            pltpu.VMEM((total, d), BF16),
            pltpu.VMEM((total, d), BF16),
            pltpu.VMEM((d, total), BF16),
            pltpu.VMEM((d, total), BF16),
            pltpu.VMEM((total, heads * block), F32),
            pltpu.VMEM((total, heads * block), BF16),
            pltpu.VMEM((total, d), F32),
            pltpu.VMEM((total, d), F32),
            pltpu.VMEM((ns, nb, 2 * rows, d // 2 + LANES), BF16),
            pltpu.VMEM((nb, 2 * rows, d // 2), BF16),
            pltpu.VMEM((nb, 2 * rows, d // 2), BF16),
            dma((5,)),
            dma((nb,)),
            dma((nb,)),
            dma((ns,)),
            dma((ns,)),
            dma((nb,)),
            dma((nb,)),
        ],
        compiler_params=pltpu.CompilerParams(
            collective_id=0, has_side_effects=True, vmem_limit_bytes=36 * 2**20
        ),
        name="pairs",
    )(
        captions,
        owner.reshape(rows, 1),
        image_tokens.reshape(total, d),
        w_query,
        w_key,
        w_value,
        w_out,
    )
    caption_grad, token_grad = pl.pallas_call(
        functools.partial(token_kernel, patches),
        out_shape=(
            jax.ShapeDtypeStruct((rows, d), F32),
            jax.ShapeDtypeStruct((total, d), F32),
        ),
        in_specs=[vmem] * 5,
        out_specs=(vmem, vmem),
        compiler_params=pltpu.CompilerParams(vmem_limit_bytes=16 * 2**20),
        name="token_grad",
    )(summed, gk, gv, w_key, w_value)
    return (caption_grad, token_grad.reshape(images, patches, d))


def solution(mesh):
    placed = (
        P("batch", None, None),
        P(("batch", "span"), None),
        P(("batch", "span")),
        P(),
        P(),
        P(),
        P(),
    )
    return jax.shard_map(
        functools.partial(on_device, mesh.shape["batch"], mesh.shape["span"]),
        mesh=mesh,
        in_specs=placed,
        out_specs=(P(("batch", "span"), None), P("batch", None, None)),
        check_vma=False,
    )
```

```python
import functools
import math

import jax
import jax.numpy as jnp
from jax import lax
from jax.experimental import pallas as pl
from jax.experimental.pallas import tpu as pltpu
from jax.sharding import PartitionSpec as P

HEAD_DIM = 64
LOGIT_SCALE = 10.0
LOGIT_BIAS = -2.0
NORM_EPS = 1e-06
CAPTION_SCALE = 16.0
LANES = 128
GROUP = 256
HEADS_IN_GROUP = GROUP // HEAD_DIM
F32 = jnp.float32
BF16 = jnp.bfloat16
MESH = pl.DeviceIdType.MESH


def dot(a, b):
    return jnp.dot(a, b, preferred_element_type=F32)


def dot_t(a, b):
    return lax.dot_general(a, b, (((1,), (1,)), ((), ())), preferred_element_type=F32)


def head_stack(x):
    head = lax.broadcasted_iota(jnp.int32, x.shape, 1) // HEAD_DIM
    return jnp.concatenate(
        [jnp.where(head == h, x, jnp.zeros_like(x)) for h in range(HEADS_IN_GROUP)], axis=0
    )


def head_blocks(x, width):
    return jnp.concatenate(
        [
            x[h * HEAD_DIM : (h + 1) * HEAD_DIM, h * width : (h + 1) * width]
            for h in range(HEADS_IN_GROUP)
        ],
        axis=0,
    )


def head_columns(parts, width):
    parts = [
        part[:, h * width : (h + 1) * width] for part in parts for h in range(HEADS_IN_GROUP)
    ]
    return jnp.concatenate(
        [jnp.broadcast_to(part, (HEAD_DIM, width)) for part in parts], axis=0
    ).T


def pair_kernel(
    nb,
    ns,
    images,
    captions_hbm,
    owner_hbm,
    tokens_hbm,
    wq_hbm,
    wk_hbm,
    wv_hbm,
    wo_hbm,
    gk_out,
    gv_out,
    sum_out,
    wk,
    wv,
    captions_ref,
    owner_ref,
    tokens,
    wq,
    wo,
    keys,
    values,
    keys_t,
    values_t,
    weights_ref,
    gk,
    gv,
    caps,
    owners,
    part,
    parts_in,
    load_sem,
    cap_send,
    cap_recv,
    owner_send,
    owner_recv,
    span_send,
    span_recv,
    span_owner_send,
    span_owner_recv,
    part_send,
    part_recv,
):
    me = lax.axis_index("batch")
    my_span = lax.axis_index("span")
    rows = captions_ref.shape[0]
    d = captions_ref.shape[1]
    half = d // 2
    patches = tokens.shape[0] // images
    groups = d // GROUP
    block = math.gcd(nb * rows, LANES)
    slots = block // rows
    blocks = nb * rows // block
    stacked = HEADS_IN_GROUP * block

    def peer_of(step):
        return lax.rem(me + step, nb)

    def span_of(step):
        return lax.rem(my_span + step, ns)

    loads = [
        pltpu.make_async_copy(src, dst, load_sem.at[n])
        for n, (src, dst) in enumerate(
            (
                (captions_hbm, captions_ref),
                (owner_hbm, owner_ref),
                (tokens_hbm, tokens),
                (wk_hbm, wk),
                (wv_hbm, wv),
                (wq_hbm, wq),
                (wo_hbm, wo),
            )
        )
    ]
    for load in loads[:2]:
        load.start()

    barrier = pltpu.get_barrier_semaphore()

    @pl.loop(1, nb)
    def _(step):
        pl.semaphore_signal(
            barrier, inc=1, device_id={"batch": peer_of(step)}, device_id_type=MESH
        )

    for step in range(1, ns):
        pl.semaphore_signal(
            barrier, inc=1, device_id={"span": span_of(step)}, device_id_type=MESH
        )

    for load in loads[2:]:
        load.start()
    for load in loads[:2]:
        load.wait()
    mine = captions_ref[...].astype(F32)
    caps[0, me] = jnp.concatenate([mine[:, :half], mine[:, half:]], axis=0).astype(BF16)
    owners[0, me] = jnp.concatenate(
        [owner_ref[...], jnp.zeros((1, LANES - rows), jnp.int32)], axis=1
    )

    pl.semaphore_wait(barrier, nb + ns - 2)

    def cap_copy(step, slot):
        return pltpu.make_async_remote_copy(
            src_ref=caps.at[0, me],
            dst_ref=caps.at[0, me],
            send_sem=cap_send.at[step],
            recv_sem=cap_recv.at[slot],
            device_id={"batch": peer_of(step)},
            device_id_type=MESH,
        )

    def owner_copy(step, slot):
        return pltpu.make_async_remote_copy(
            src_ref=owners.at[0, me],
            dst_ref=owners.at[0, me],
            send_sem=owner_send.at[step],
            recv_sem=owner_recv.at[slot],
            device_id={"batch": peer_of(step)},
            device_id_type=MESH,
        )

    def part_copy(step, slot):
        return pltpu.make_async_remote_copy(
            src_ref=part.at[peer_of(step)],
            dst_ref=parts_in.at[me],
            send_sem=part_send.at[step],
            recv_sem=part_recv.at[slot],
            device_id={"batch": peer_of(step)},
            device_id_type=MESH,
        )

    def span_copy(step, slot):
        return pltpu.make_async_remote_copy(
            src_ref=caps.at[0],
            dst_ref=caps.at[ns - step],
            send_sem=span_send.at[step],
            recv_sem=span_recv.at[slot],
            device_id={"span": span_of(step)},
            device_id_type=MESH,
        )

    def span_owner_copy(step, slot):
        return pltpu.make_async_remote_copy(
            src_ref=owners.at[0],
            dst_ref=owners.at[ns - step],
            send_sem=span_owner_send.at[step],
            recv_sem=span_owner_recv.at[slot],
            device_id={"span": span_of(step)},
            device_id_type=MESH,
        )

    @pl.loop(1, nb)
    def _(step):
        cap_copy(step, me).start()

    @pl.loop(1, nb)
    def _(step):
        owner_copy(step, me).start()

    for load in loads[2:5]:
        load.wait()
    for i in range(images):
        at = pl.ds(i * patches, patches)
        found = dot(tokens[at, :], wk[...])
        keys[at, :] = found.astype(BF16)
        keys_t[:, at] = found.T.astype(BF16)
        found = dot(tokens[at, :], wv[...])
        values[at, :] = found.astype(BF16)
        values_t[:, at] = found.T.astype(BF16)
    gk[...] = jnp.zeros_like(gk)
    gv[...] = jnp.zeros_like(gv)
    for load in loads[5:]:
        load.wait()

    @pl.loop(1, nb)
    def _(step):
        cap_copy(step, peer_of(step)).wait_recv()

    for step in range(1, ns):
        span_copy(step, ns - step).start()

    @pl.loop(1, nb)
    def _(step):
        owner_copy(step, peer_of(step)).wait_recv()

    for step in range(1, ns):
        span_owner_copy(step, ns - step).start()

    def run_block(slot, which, own):
        held = caps[which, pl.ds(slot, slots)].astype(F32)
        caption = jnp.concatenate(
            [
                held[:, :rows].reshape(block, half),
                held[:, rows:].reshape(block, half),
            ],
            axis=1,
        )
        owner = owners[which, pl.ds(slot, slots)]
        owner = jnp.broadcast_to(owner, (slots, rows, LANES))
        row = lax.broadcasted_iota(jnp.int32, owner.shape, 1)
        lane = lax.broadcasted_iota(jnp.int32, owner.shape, 2)
        owner = jnp.sum(
            jnp.where(row == lane, owner, 0).astype(F32).reshape(block, LANES),
            axis=1,
            keepdims=True,
        )
        query = (dot(caption.astype(BF16), wq[...]) * HEAD_DIM**-0.5).astype(BF16)
        queries = [head_stack(query[:, g * GROUP : (g + 1) * GROUP]) for g in range(groups)]

        pooled = []
        inverse = []
        for i in range(images):
            at = slice(i * patches, (i + 1) * patches)
            found = []
            inverse.append([])
            for g in range(groups):
                cols = slice(g * GROUP, (g + 1) * GROUP)
                to = slice(g * stacked, (g + 1) * stacked)
                scores = dot_t(keys[at, cols], queries[g])
                scores = jnp.exp(scores - jnp.max(scores, axis=0, keepdims=True))
                inverse[i].append(1.0 / jnp.sum(scores, axis=0, keepdims=True))
                weights = scores.astype(BF16)
                weights_ref[at, to] = weights
                found.append(
                    head_blocks(dot(values_t[cols, at], weights) * inverse[i][g], block)
                )
            pooled.append(jnp.concatenate(found, axis=0).T.astype(BF16))
        mixed = dot(jnp.concatenate(pooled, axis=0), wo[...])
        caption_2 = jnp.concatenate([caption] * images, axis=0)
        owner_2 = jnp.concatenate([owner] * images, axis=0)
        image = (
            lax.broadcasted_iota(jnp.int32, (images * block, 1), 0) // block + me * images
        ).astype(F32)
        inner = jnp.sum(mixed * caption_2, axis=1, keepdims=True)
        mixed_inv = lax.rsqrt(jnp.sum(mixed * mixed, axis=1, keepdims=True) + NORM_EPS)
        caption_inv = lax.rsqrt(jnp.sum(caption * caption, axis=1, keepdims=True) + NORM_EPS)
        caption_inv = jnp.concatenate([caption_inv] * images, axis=0)
        cosine = inner * mixed_inv * caption_inv
        logit = LOGIT_SCALE * cosine + LOGIT_BIAS
        label = jnp.where(owner_2 == image, 1.0, -1.0)
        slope = -LOGIT_SCALE * label / (1.0 + jnp.exp(label * logit))
        across = slope * mixed_inv * caption_inv
        grad_mixed = across * caption_2 - (slope * cosine * mixed_inv * mixed_inv) * mixed
        by_caption = jnp.concatenate([head_columns(rows_, block) for rows_ in inverse], axis=0)
        grad_pooled = (dot_t(grad_mixed.astype(BF16), wo[...]) * by_caption).astype(BF16)
        if own:
            direct = across * mixed - (slope * cosine * caption_inv * caption_inv) * caption_2
            direct = sum(direct[i * block : (i + 1) * block] for i in range(images))

        grad_query = []
        for g in range(groups):
            cols = slice(g * GROUP, (g + 1) * GROUP)
            to = slice(g * stacked, (g + 1) * stacked)
            total = None
            for i in range(images):
                at = slice(i * patches, (i + 1) * patches)
                grads = head_stack(grad_pooled[i * block : (i + 1) * block, cols])
                grad_weights = dot_t(values[at, cols], grads)
                gv[at, cols] += dot(weights_ref[at, to], grads)
                weights = weights_ref[at, to].astype(F32)
                mean = jnp.sum(weights * grad_weights, axis=0, keepdims=True) * inverse[i][g]
                grad_scores = weights * (grad_weights - mean)
                grad_scores = grad_scores.astype(BF16)
                gk[at, cols] += dot(grad_scores, queries[g])
                if own:
                    found = head_blocks(dot(keys_t[cols, at], grad_scores), block)
                    total = found if total is None else total + found
            grad_query.append(total)
        if own:
            grad_query = jnp.concatenate(grad_query, axis=0).T * HEAD_DIM**-0.5
            grad = direct + dot_t(grad_query.astype(BF16), wq[...])
            grad = grad.reshape(slots, rows, d)
            part[pl.ds(slot, slots)] = jnp.concatenate(
                [grad[:, :, :half], grad[:, :, half:]], axis=1
            ).astype(BF16)

    def run_all(which, own):
        if blocks == 1:
            run_block(0, which, own)
        else:

            @pl.loop(0, blocks)
            def _(n):
                run_block(n * slots, which, own)

    run_all(0, True)

    @pl.loop(1, nb)
    def _(step):
        part_copy(step, me).start()

    for step in range(1, ns):
        span_copy(step, step).wait_recv()
        span_owner_copy(step, step).wait_recv()
        run_all(step, False)

    gk_out[...] = gk[...].astype(BF16)
    gv_out[...] = gv[...].astype(BF16)

    @pl.loop(1, nb)
    def _(step):
        part_copy(step, peer_of(step)).wait_recv()

    parts_in[me] = part[me]
    sum_out[...] = jnp.sum(parts_in[...].astype(F32), axis=0)

    @pl.loop(1, nb)
    def _(step):
        cap_copy(step, me).wait_send()
        owner_copy(step, me).wait_send()
        part_copy(step, me).wait_send()

    for step in range(1, ns):
        span_copy(step, ns - step).wait_send()
        span_owner_copy(step, ns - step).wait_send()


def token_kernel(patches, sum_ref, gk, gv, wk, wv, caption_out, token_out, made, sems):
    rows, d = caption_out.shape
    total = gk.shape[0]
    chunk = math.gcd(total, LANES)
    copies = []
    for n in range(total // chunk):
        at = pl.ds(n * chunk, chunk)
        made[at, :] = patches * (dot_t(gk[at, :], wk[...]) + dot_t(gv[at, :], wv[...]))
        copies.append(pltpu.make_async_copy(made.at[at], token_out.at[at], sems.at[n]))
        copies[-1].start()
    summed = sum_ref[...] * CAPTION_SCALE
    caption_out[...] = jnp.concatenate([summed[:rows], summed[rows:]], axis=1)
    for copy in copies:
        copy.wait()


def hold(x):
    return pltpu.with_memory_space_constraint(x, pltpu.HBM)


def on_device(nb, ns, image_tokens, captions, owner, w_query, w_key, w_value, w_out):
    images, patches, d = image_tokens.shape
    rows = captions.shape[0]
    total = images * patches
    block = math.gcd(nb * rows, LANES)
    vmem = pl.BlockSpec(memory_space=pltpu.VMEM)
    hbm = pl.BlockSpec(memory_space=pltpu.HBM)
    heads = d // HEAD_DIM
    dma = pltpu.SemaphoreType.DMA
    gk, gv, summed, wk, wv = pl.pallas_call(
        functools.partial(pair_kernel, nb, ns, images),
        out_shape=(
            jax.ShapeDtypeStruct((total, d), BF16),
            jax.ShapeDtypeStruct((total, d), BF16),
            jax.ShapeDtypeStruct((2 * rows, d // 2), F32),
            jax.ShapeDtypeStruct((d, d), BF16),
            jax.ShapeDtypeStruct((d, d), BF16),
        ),
        in_specs=[hbm] * 7,
        out_specs=(vmem,) * 5,
        scratch_shapes=[
            pltpu.VMEM((rows, d), BF16),
            pltpu.VMEM((1, rows), jnp.int32),
            pltpu.VMEM((total, d), BF16),
            pltpu.VMEM((d, d), BF16),
            pltpu.VMEM((d, d), BF16),
            pltpu.VMEM((total, d), BF16),
            pltpu.VMEM((total, d), BF16),
            pltpu.VMEM((d, total), BF16),
            pltpu.VMEM((d, total), BF16),
            pltpu.VMEM((total, heads * block), BF16),
            pltpu.VMEM((total, d), F32),
            pltpu.VMEM((total, d), F32),
            pltpu.VMEM((ns, nb, 2 * rows, d // 2), BF16),
            pltpu.VMEM((ns, nb, 1, LANES), jnp.int32),
            pltpu.VMEM((nb, 2 * rows, d // 2), BF16),
            pltpu.VMEM((nb, 2 * rows, d // 2), BF16),
            dma((7,)),
            dma((nb,)),
            dma((nb,)),
            dma((nb,)),
            dma((nb,)),
            dma((ns,)),
            dma((ns,)),
            dma((ns,)),
            dma((ns,)),
            dma((nb,)),
            dma((nb,)),
        ],
        compiler_params=pltpu.CompilerParams(
            collective_id=0, has_side_effects=True, vmem_limit_bytes=36 * 2**20
        ),
        name="pairs",
    )(
        hold(captions),
        hold(owner.reshape(1, rows)),
        hold(image_tokens.reshape(total, d)),
        hold(w_query),
        hold(w_key),
        hold(w_value),
        hold(w_out),
    )
    caption_grad, token_grad = pl.pallas_call(
        functools.partial(token_kernel, patches),
        out_shape=(
            jax.ShapeDtypeStruct((rows, d), F32),
            jax.ShapeDtypeStruct((total, d), F32),
        ),
        in_specs=[vmem] * 5,
        out_specs=(vmem, hbm),
        scratch_shapes=[
            pltpu.VMEM((total, d), F32),
            dma((total // math.gcd(total, LANES),)),
        ],
        compiler_params=pltpu.CompilerParams(vmem_limit_bytes=16 * 2**20),
        name="token_grad",
    )(summed, gk, gv, wk, wv)
    return (caption_grad, token_grad.reshape(images, patches, d))


def solution(mesh):
    placed = (
        P("batch", None, None),
        P(("batch", "span"), None),
        P(("batch", "span")),
        P(),
        P(),
        P(),
        P(),
    )
    return jax.shard_map(
        functools.partial(on_device, mesh.shape["batch"], mesh.shape["span"]),
        mesh=mesh,
        in_specs=placed,
        out_specs=(P(("batch", "span"), None), P("batch", None, None)),
        check_vma=False,
    )
```

```python
import functools
import math

import jax
import jax.numpy as jnp
from jax import lax
from jax.experimental import pallas as pl
from jax.experimental.pallas import tpu as pltpu
from jax.sharding import PartitionSpec as P

HEAD_DIM = 64
LOGIT_SCALE = 10.0
LOGIT_BIAS = -2.0
NORM_EPS = 1e-06
CAPTION_SCALE = 16.0
LANES = 128
GROUP = 256
HEADS_IN_GROUP = GROUP // HEAD_DIM
F32 = jnp.float32
BF16 = jnp.bfloat16
MESH = pl.DeviceIdType.MESH


def dot(a, b):
    return jnp.dot(a, b, preferred_element_type=F32)


def dot_t(a, b):
    return lax.dot_general(a, b, (((1,), (1,)), ((), ())), preferred_element_type=F32)


def head_stack(x):
    head = lax.broadcasted_iota(jnp.int32, x.shape, 1) // HEAD_DIM
    return jnp.concatenate(
        [jnp.where(head == h, x, jnp.zeros_like(x)) for h in range(HEADS_IN_GROUP)], axis=0
    )


def head_blocks(x, width):
    return jnp.concatenate(
        [
            x[h * HEAD_DIM : (h + 1) * HEAD_DIM, h * width : (h + 1) * width]
            for h in range(HEADS_IN_GROUP)
        ],
        axis=0,
    )


def head_columns(parts, width):
    parts = [
        part[:, h * width : (h + 1) * width] for part in parts for h in range(HEADS_IN_GROUP)
    ]
    return jnp.concatenate(
        [jnp.broadcast_to(part, (HEAD_DIM, width)) for part in parts], axis=0
    ).T


def pair_kernel(
    nb,
    ns,
    images,
    captions_hbm,
    owner_hbm,
    tokens_hbm,
    wq_hbm,
    wk_hbm,
    wv_hbm,
    wo_hbm,
    gk_out,
    gv_out,
    sum_out,
    wk,
    wv,
    captions_ref,
    owner_ref,
    tokens,
    wq,
    wo,
    keys,
    values,
    keys_t,
    values_t,
    weights_ref,
    gk,
    gv,
    caps,
    owners,
    part,
    parts_in,
    load_sem,
    cap_send,
    cap_recv,
    owner_send,
    owner_recv,
    span_send,
    span_recv,
    span_owner_send,
    span_owner_recv,
    part_send,
    part_recv,
):
    me = lax.axis_index("batch")
    my_span = lax.axis_index("span")
    rows = captions_ref.shape[0]
    d = captions_ref.shape[1]
    half = d // 2
    patches = tokens.shape[0] // images
    groups = d // GROUP
    block = math.gcd(nb * rows, LANES)
    slots = block // rows
    blocks = nb * rows // block
    stacked = HEADS_IN_GROUP * block
    unroll = nb <= 16

    def peer_of(step):
        return lax.rem(me + step, nb)

    def span_of(step):
        return lax.rem(my_span + step, ns)

    loads = [
        pltpu.make_async_copy(src, dst, load_sem.at[n])
        for n, (src, dst) in enumerate(
            (
                (captions_hbm, captions_ref),
                (owner_hbm, owner_ref),
                (tokens_hbm, tokens),
                (wk_hbm, wk),
                (wv_hbm, wv),
                (wq_hbm, wq),
                (wo_hbm, wo),
            )
        )
    ]
    for load in loads[:2]:
        load.start()

    barrier = pltpu.get_barrier_semaphore()

    @pl.loop(1, nb, unroll=unroll)
    def _(step):
        pl.semaphore_signal(
            barrier, inc=1, device_id={"batch": peer_of(step)}, device_id_type=MESH
        )

    for step in range(1, ns):
        pl.semaphore_signal(
            barrier, inc=1, device_id={"span": span_of(step)}, device_id_type=MESH
        )

    for load in loads[2:]:
        load.start()
    for load in loads[:2]:
        load.wait()
    mine = captions_ref[...].astype(F32)
    caps[0, me] = jnp.concatenate([mine[:, :half], mine[:, half:]], axis=0).astype(BF16)
    owners[0, me] = jnp.concatenate(
        [owner_ref[...], jnp.zeros((1, LANES - rows), jnp.int32)], axis=1
    )

    pl.semaphore_wait(barrier, nb + ns - 2)

    def cap_copy(step):
        return pltpu.make_async_remote_copy(
            src_ref=caps.at[0, me],
            dst_ref=caps.at[0, me],
            send_sem=cap_send,
            recv_sem=cap_recv,
            device_id={"batch": peer_of(step)},
            device_id_type=MESH,
        )

    def owner_copy(step):
        return pltpu.make_async_remote_copy(
            src_ref=owners.at[0, me],
            dst_ref=owners.at[0, me],
            send_sem=owner_send,
            recv_sem=owner_recv,
            device_id={"batch": peer_of(step)},
            device_id_type=MESH,
        )

    def part_copy(step):
        return pltpu.make_async_remote_copy(
            src_ref=part.at[peer_of(step)],
            dst_ref=parts_in.at[me],
            send_sem=part_send,
            recv_sem=part_recv,
            device_id={"batch": peer_of(step)},
            device_id_type=MESH,
        )

    def span_copy(step, slot):
        return pltpu.make_async_remote_copy(
            src_ref=caps.at[0],
            dst_ref=caps.at[ns - step],
            send_sem=span_send.at[step],
            recv_sem=span_recv.at[slot],
            device_id={"span": span_of(step)},
            device_id_type=MESH,
        )

    def whole(ref, send_sem, recv_sem):
        return pltpu.make_async_remote_copy(
            src_ref=ref.at[pl.ds(0, nb - 1)],
            dst_ref=ref.at[pl.ds(0, nb - 1)],
            send_sem=send_sem,
            recv_sem=recv_sem,
            device_id={"batch": peer_of(1)},
            device_id_type=MESH,
        )

    all_caps = whole(caps.at[0], cap_send, cap_recv)
    all_owners = whole(owners.at[0], owner_send, owner_recv)
    all_parts = whole(parts_in, part_send, part_recv)

    def span_owner_copy(step, slot):
        return pltpu.make_async_remote_copy(
            src_ref=owners.at[0],
            dst_ref=owners.at[ns - step],
            send_sem=span_owner_send.at[step],
            recv_sem=span_owner_recv.at[slot],
            device_id={"span": span_of(step)},
            device_id_type=MESH,
        )

    @pl.loop(1, nb, unroll=unroll)
    def _(step):
        cap_copy(step).start()

    @pl.loop(1, nb, unroll=unroll)
    def _(step):
        owner_copy(step).start()

    for load in loads[2:5]:
        load.wait()
    for i in range(images):
        at = pl.ds(i * patches, patches)
        found = dot(tokens[at, :], wk[...])
        keys[at, :] = found.astype(BF16)
        keys_t[:, at] = found.T.astype(BF16)
        found = dot(tokens[at, :], wv[...])
        values[at, :] = found.astype(BF16)
        values_t[:, at] = found.T.astype(BF16)
    if blocks > 1:
        gk[...] = jnp.zeros_like(gk)
        gv[...] = jnp.zeros_like(gv)
    for load in loads[5:]:
        load.wait()

    all_caps.wait_recv()

    for step in range(1, ns):
        span_copy(step, ns - step).start()

    all_owners.wait_recv()

    for step in range(1, ns):
        span_owner_copy(step, ns - step).start()

    def add(total, out, at, cols, found, which):
        if blocks > 1 or which > 0:
            found = total[at, cols] + found
        if blocks == 1 and which == ns - 1:
            out[at, cols] = found.astype(BF16)
        else:
            total[at, cols] = found

    def run_block(slot, which, own):
        later = []
        held = caps[which, pl.ds(slot, slots)].astype(F32)
        caption = jnp.concatenate(
            [
                held[:, :rows].reshape(block, half),
                held[:, rows:].reshape(block, half),
            ],
            axis=1,
        )
        owner = owners[which, pl.ds(slot, slots)]
        owner = jnp.broadcast_to(owner, (slots, rows, LANES))
        row = lax.broadcasted_iota(jnp.int32, owner.shape, 1)
        lane = lax.broadcasted_iota(jnp.int32, owner.shape, 2)
        owner = jnp.sum(
            jnp.where(row == lane, owner, 0).astype(F32).reshape(block, LANES),
            axis=1,
            keepdims=True,
        )
        query = (dot(caption.astype(BF16), wq[...]) * HEAD_DIM**-0.5).astype(BF16)
        queries = [head_stack(query[:, g * GROUP : (g + 1) * GROUP]) for g in range(groups)]

        pooled = []
        inverse = []
        for i in range(images):
            at = slice(i * patches, (i + 1) * patches)
            found = []
            inverse.append([])
            for g in range(groups):
                cols = slice(g * GROUP, (g + 1) * GROUP)
                to = slice(g * stacked, (g + 1) * stacked)
                scores = dot_t(keys[at, cols], queries[g])
                scores = jnp.exp(scores - jnp.max(scores, axis=0, keepdims=True))
                inverse[i].append(1.0 / jnp.sum(scores, axis=0, keepdims=True))
                weights = scores.astype(BF16)
                weights_ref[which, at, to] = weights
                found.append(
                    head_blocks(dot(values_t[cols, at], weights) * inverse[i][g], block)
                )
            pooled.append(jnp.concatenate(found, axis=0).T.astype(BF16))
        mixed = dot(jnp.concatenate(pooled, axis=0), wo[...])
        caption_2 = jnp.concatenate([caption] * images, axis=0)
        owner_2 = jnp.concatenate([owner] * images, axis=0)
        image = (
            lax.broadcasted_iota(jnp.int32, (images * block, 1), 0) // block + me * images
        ).astype(F32)
        inner = jnp.sum(mixed * caption_2, axis=1, keepdims=True)
        mixed_inv = lax.rsqrt(jnp.sum(mixed * mixed, axis=1, keepdims=True) + NORM_EPS)
        caption_inv = lax.rsqrt(jnp.sum(caption * caption, axis=1, keepdims=True) + NORM_EPS)
        caption_inv = jnp.concatenate([caption_inv] * images, axis=0)
        cosine = inner * mixed_inv * caption_inv
        logit = LOGIT_SCALE * cosine + LOGIT_BIAS
        label = jnp.where(owner_2 == image, 1.0, -1.0)
        slope = -LOGIT_SCALE * label / (1.0 + jnp.exp(label * logit))
        across = slope * mixed_inv * caption_inv
        grad_mixed = across * caption_2 - (slope * cosine * mixed_inv * mixed_inv) * mixed
        by_caption = jnp.concatenate([head_columns(rows_, block) for rows_ in inverse], axis=0)
        grad_pooled = (dot_t(grad_mixed.astype(BF16), wo[...]) * by_caption).astype(BF16)
        if own:
            direct = across * mixed - (slope * cosine * caption_inv * caption_inv) * caption_2
            direct = sum(direct[i * block : (i + 1) * block] for i in range(images))

        grad_query = []
        for g in range(groups):
            cols = slice(g * GROUP, (g + 1) * GROUP)
            to = slice(g * stacked, (g + 1) * stacked)
            total = None
            for i in range(images):
                at = slice(i * patches, (i + 1) * patches)
                grads = head_stack(grad_pooled[i * block : (i + 1) * block, cols])
                grad_weights = dot_t(values[at, cols], grads)
                weights = weights_ref[which, at, to].astype(F32)
                mean = jnp.sum(weights * grad_weights, axis=0, keepdims=True) * inverse[i][g]
                grad_scores = weights * (grad_weights - mean)
                grad_scores = grad_scores.astype(BF16)
                later.append(
                    functools.partial(
                        finish, at, cols, to, grads, grad_scores, queries[g], which
                    )
                )
                if own:
                    found = head_blocks(dot(keys_t[cols, at], grad_scores), block)
                    total = found if total is None else total + found
            grad_query.append(total)
        if own:
            grad_query = jnp.concatenate(grad_query, axis=0).T * HEAD_DIM**-0.5
            grad = direct + dot_t(grad_query.astype(BF16), wq[...])
            grad = grad.reshape(slots, rows, d)
            part[pl.ds(slot, slots)] = jnp.concatenate(
                [grad[:, :, :half], grad[:, :, half:]], axis=1
            ).astype(BF16)
        return later

    def finish(at, cols, to, grads, grad_scores, queries, which):
        add(gv, gv_out, at, cols, dot(weights_ref[which, at, to], grads), which)
        add(gk, gk_out, at, cols, dot(grad_scores, queries), which)

    def run_all(which, own):
        if blocks == 1:
            return run_block(0, which, own)

        @pl.loop(0, blocks)
        def _(n):
            for work in run_block(n * slots, which, own):
                work()

        return []

    later = run_all(0, True)

    @pl.loop(1, nb, unroll=unroll)
    def _(step):
        part_copy(step).start()

    for step in range(1, ns):
        span_copy(step, step).wait_recv()
        span_owner_copy(step, step).wait_recv()
        for work in later:
            work()
        later = run_all(step, False)
    for work in later:
        work()
    if blocks > 1:
        gk_out[...] = gk[...].astype(BF16)
        gv_out[...] = gv[...].astype(BF16)

    all_parts.wait_recv()

    parts_in[me] = part[me]
    sum_out[...] = jnp.sum(parts_in[...].astype(F32), axis=0)

    all_caps.wait_send()
    all_owners.wait_send()
    all_parts.wait_send()

    for step in range(1, ns):
        span_copy(step, ns - step).wait_send()
        span_owner_copy(step, ns - step).wait_send()


def token_kernel(patches, sum_ref, gk, gv, wk, wv, caption_out, token_out, made, sems):
    rows, d = caption_out.shape
    copies = []
    for n in range(d // GROUP):
        at = pl.ds(n * GROUP, GROUP)
        made[:, at] = patches * (dot_t(gk[...], wk[at, :]) + dot_t(gv[...], wv[at, :]))
        copies.append(pltpu.make_async_copy(made.at[:, at], token_out.at[:, at], sems.at[n]))
        copies[-1].start()
    summed = sum_ref[...] * CAPTION_SCALE
    caption_out[...] = jnp.concatenate([summed[:rows], summed[rows:]], axis=1)
    for copy in copies:
        copy.wait()


def hold(x):
    return pltpu.with_memory_space_constraint(x, pltpu.HBM)


def on_device(nb, ns, image_tokens, captions, owner, w_query, w_key, w_value, w_out):
    images, patches, d = image_tokens.shape
    rows = captions.shape[0]
    total = images * patches
    block = math.gcd(nb * rows, LANES)
    vmem = pl.BlockSpec(memory_space=pltpu.VMEM)
    hbm = pl.BlockSpec(memory_space=pltpu.HBM)
    heads = d // HEAD_DIM
    dma = pltpu.SemaphoreType.DMA
    gk, gv, summed, wk, wv = pl.pallas_call(
        functools.partial(pair_kernel, nb, ns, images),
        out_shape=(
            jax.ShapeDtypeStruct((total, d), BF16),
            jax.ShapeDtypeStruct((total, d), BF16),
            jax.ShapeDtypeStruct((2 * rows, d // 2), F32),
            jax.ShapeDtypeStruct((d, d), BF16),
            jax.ShapeDtypeStruct((d, d), BF16),
        ),
        in_specs=[hbm] * 7,
        out_specs=(vmem,) * 5,
        scratch_shapes=[
            pltpu.VMEM((rows, d), BF16),
            pltpu.VMEM((1, rows), jnp.int32),
            pltpu.VMEM((total, d), BF16),
            pltpu.VMEM((d, d), BF16),
            pltpu.VMEM((d, d), BF16),
            pltpu.VMEM((total, d), BF16),
            pltpu.VMEM((total, d), BF16),
            pltpu.VMEM((d, total), BF16),
            pltpu.VMEM((d, total), BF16),
            pltpu.VMEM((ns, total, heads * block), BF16),
            pltpu.VMEM((total, d), F32),
            pltpu.VMEM((total, d), F32),
            pltpu.VMEM((ns, nb, 2 * rows, d // 2), BF16),
            pltpu.VMEM((ns, nb, 1, LANES), jnp.int32),
            pltpu.VMEM((nb, 2 * rows, d // 2), BF16),
            pltpu.VMEM((nb, 2 * rows, d // 2), BF16),
            dma((7,)),
            dma,
            dma,
            dma,
            dma,
            dma((ns,)),
            dma((ns,)),
            dma((ns,)),
            dma((ns,)),
            dma,
            dma,
        ],
        compiler_params=pltpu.CompilerParams(
            collective_id=0, has_side_effects=True, vmem_limit_bytes=36 * 2**20
        ),
        name="pairs",
    )(
        hold(captions),
        hold(owner.reshape(1, rows)),
        hold(image_tokens.reshape(total, d)),
        hold(w_query),
        hold(w_key),
        hold(w_value),
        hold(w_out),
    )
    caption_grad, token_grad = pl.pallas_call(
        functools.partial(token_kernel, patches),
        out_shape=(
            jax.ShapeDtypeStruct((rows, d), F32),
            jax.ShapeDtypeStruct((total, d), F32),
        ),
        in_specs=[vmem] * 5,
        out_specs=(vmem, hbm),
        scratch_shapes=[
            pltpu.VMEM((total, d), F32),
            dma((d // GROUP,)),
        ],
        compiler_params=pltpu.CompilerParams(vmem_limit_bytes=16 * 2**20),
        name="token_grad",
    )(summed, gk, gv, wk, wv)
    return (caption_grad, token_grad.reshape(images, patches, d))


def solution(mesh):
    placed = (
        P("batch", None, None),
        P(("batch", "span"), None),
        P(("batch", "span")),
        P(),
        P(),
        P(),
        P(),
    )
    return jax.shard_map(
        functools.partial(on_device, mesh.shape["batch"], mesh.shape["span"]),
        mesh=mesh,
        in_specs=placed,
        out_specs=(P(("batch", "span"), None), P("batch", None, None)),
        check_vma=False,
    )
```

```python
import functools
import math

import jax
import jax.numpy as jnp
from jax import lax
from jax.experimental import pallas as pl
from jax.experimental.pallas import tpu as pltpu
from jax.sharding import PartitionSpec as P

HEAD_DIM = 64
LOGIT_SCALE = 10.0
LOGIT_BIAS = -2.0
NORM_EPS = 1e-06
CAPTION_SCALE = 16.0
LANES = 128
GROUP = 256
HEADS_IN_GROUP = GROUP // HEAD_DIM
F32 = jnp.float32
BF16 = jnp.bfloat16
MESH = pl.DeviceIdType.MESH


def dot(a, b):
    return jnp.dot(a, b, preferred_element_type=F32)


def dot_t(a, b):
    return lax.dot_general(a, b, (((1,), (1,)), ((), ())), preferred_element_type=F32)


def head_masks(tile):
    head = lax.broadcasted_iota(jnp.int32, (tile, GROUP), 1) // HEAD_DIM
    return [(head == h).astype(F32).astype(BF16) for h in range(HEADS_IN_GROUP)]


def head_stack(x):
    tile = math.gcd(x.shape[0], 16)
    tiles = x.reshape(x.shape[0] // tile, tile, GROUP)
    return jnp.concatenate([(tiles * m).reshape(x.shape) for m in head_masks(tile)], axis=0)


def head_blocks(x, width):
    return jnp.concatenate(
        [
            x[h * HEAD_DIM : (h + 1) * HEAD_DIM, h * width : (h + 1) * width]
            for h in range(HEADS_IN_GROUP)
        ],
        axis=0,
    )


def head_columns(parts, width):
    parts = [
        part[:, h * width : (h + 1) * width] for part in parts for h in range(HEADS_IN_GROUP)
    ]
    return jnp.concatenate(
        [jnp.broadcast_to(part, (HEAD_DIM, width)) for part in parts], axis=0
    ).T


def pair_kernel(
    nb,
    ns,
    images,
    captions_hbm,
    owner_hbm,
    tokens_hbm,
    wq_hbm,
    wk_hbm,
    wv_hbm,
    wo_hbm,
    gk_out,
    gv_out,
    sum_out,
    wk,
    wv,
    captions_ref,
    owner_ref,
    tokens,
    wq,
    wo,
    keys,
    values,
    keys_t,
    values_t,
    weights_ref,
    gk,
    gv,
    caps,
    owners,
    part,
    parts_in,
    load_sem,
    cap_send,
    cap_recv,
    owner_send,
    owner_recv,
    span_send,
    span_recv,
    span_owner_send,
    span_owner_recv,
    part_send,
    part_recv,
):
    me = lax.axis_index("batch")
    my_span = lax.axis_index("span")
    rows = captions_ref.shape[0]
    d = captions_ref.shape[1]
    half = d // 2
    patches = tokens.shape[0] // images
    groups = d // GROUP
    block = math.gcd(nb * rows, LANES)
    slots = block // rows
    blocks = nb * rows // block
    stacked = HEADS_IN_GROUP * block
    unroll = nb <= 16

    def peer_of(step):
        return lax.rem(me + step, nb)

    def span_of(step):
        return lax.rem(my_span + step, ns)

    loads = [
        pltpu.make_async_copy(src, dst, load_sem.at[n])
        for n, (src, dst) in enumerate(
            (
                (captions_hbm, captions_ref),
                (owner_hbm, owner_ref),
                (tokens_hbm, tokens),
                (wk_hbm, wk),
                (wv_hbm, wv),
                (wq_hbm, wq),
                (wo_hbm, wo),
            )
        )
    ]
    for load in loads[:2]:
        load.start()

    barrier = pltpu.get_barrier_semaphore()

    @pl.loop(1, nb, unroll=unroll)
    def _(step):
        pl.semaphore_signal(
            barrier, inc=1, device_id={"batch": peer_of(step)}, device_id_type=MESH
        )

    for step in range(1, ns):
        pl.semaphore_signal(
            barrier, inc=1, device_id={"span": span_of(step)}, device_id_type=MESH
        )

    for load in loads[2:]:
        load.start()
    for load in loads[:2]:
        load.wait()
    mine = captions_ref[...].astype(F32)
    caps[0, me] = jnp.concatenate([mine[:, :half], mine[:, half:]], axis=0).astype(BF16)
    owners[0, me] = jnp.concatenate(
        [owner_ref[...], jnp.zeros((1, LANES - rows), jnp.int32)], axis=1
    )

    pl.semaphore_wait(barrier, nb + ns - 2)

    def cap_copy(step):
        return pltpu.make_async_remote_copy(
            src_ref=caps.at[0, me],
            dst_ref=caps.at[0, me],
            send_sem=cap_send,
            recv_sem=cap_recv,
            device_id={"batch": peer_of(step)},
            device_id_type=MESH,
        )

    def owner_copy(step):
        return pltpu.make_async_remote_copy(
            src_ref=owners.at[0, me],
            dst_ref=owners.at[0, me],
            send_sem=owner_send,
            recv_sem=owner_recv,
            device_id={"batch": peer_of(step)},
            device_id_type=MESH,
        )

    def part_copy(step):
        return pltpu.make_async_remote_copy(
            src_ref=part.at[peer_of(step)],
            dst_ref=parts_in.at[me],
            send_sem=part_send,
            recv_sem=part_recv,
            device_id={"batch": peer_of(step)},
            device_id_type=MESH,
        )

    def span_copy(step, slot):
        return pltpu.make_async_remote_copy(
            src_ref=caps.at[0],
            dst_ref=caps.at[ns - step],
            send_sem=span_send.at[step],
            recv_sem=span_recv.at[slot],
            device_id={"span": span_of(step)},
            device_id_type=MESH,
        )

    def whole(ref, send_sem, recv_sem):
        return pltpu.make_async_remote_copy(
            src_ref=ref.at[pl.ds(0, nb - 1)],
            dst_ref=ref.at[pl.ds(0, nb - 1)],
            send_sem=send_sem,
            recv_sem=recv_sem,
            device_id={"batch": peer_of(1)},
            device_id_type=MESH,
        )

    all_caps = whole(caps.at[0], cap_send, cap_recv)
    all_owners = whole(owners.at[0], owner_send, owner_recv)
    all_parts = whole(parts_in, part_send, part_recv)

    def span_owner_copy(step, slot):
        return pltpu.make_async_remote_copy(
            src_ref=owners.at[0],
            dst_ref=owners.at[ns - step],
            send_sem=span_owner_send.at[step],
            recv_sem=span_owner_recv.at[slot],
            device_id={"span": span_of(step)},
            device_id_type=MESH,
        )

    @pl.loop(1, nb, unroll=unroll)
    def _(step):
        cap_copy(step).start()

    @pl.loop(1, nb, unroll=unroll)
    def _(step):
        owner_copy(step).start()

    for load in loads[2:5]:
        load.wait()
    for i in range(images):
        at = pl.ds(i * patches, patches)
        found = dot(tokens[at, :], wk[...])
        keys[at, :] = found.astype(BF16)
        keys_t[:, at] = found.astype(BF16).T
        found = dot(tokens[at, :], wv[...])
        values[at, :] = found.astype(BF16)
        values_t[:, at] = found.astype(BF16).T
    if blocks > 1:
        gk[...] = jnp.zeros_like(gk)
        gv[...] = jnp.zeros_like(gv)
    for load in loads[5:]:
        load.wait()

    all_caps.wait_recv()

    for step in range(1, ns):
        span_copy(step, ns - step).start()

    all_owners.wait_recv()

    for step in range(1, ns):
        span_owner_copy(step, ns - step).start()

    def add(total, out, at, cols, found, which):
        if blocks > 1 or which > 0:
            found = total[at, cols] + found
        if blocks == 1 and which == ns - 1:
            out[at, cols] = found.astype(BF16)
        else:
            total[at, cols] = found

    def run_block(slot, which, own, before=()):
        later = []
        held = caps[which, pl.ds(slot, slots)].astype(F32)
        caption = jnp.concatenate(
            [
                held[:, :rows].reshape(block, half),
                held[:, rows:].reshape(block, half),
            ],
            axis=1,
        )
        owner = owners[which, pl.ds(slot, slots)]
        owner = jnp.broadcast_to(owner, (slots, rows, LANES))
        row = lax.broadcasted_iota(jnp.int32, owner.shape, 1)
        lane = lax.broadcasted_iota(jnp.int32, owner.shape, 2)
        owner = jnp.sum(
            jnp.where(row == lane, owner, 0).astype(F32).reshape(block, LANES),
            axis=1,
            keepdims=True,
        )
        query = (dot(caption.astype(BF16), wq[...]) * HEAD_DIM**-0.5).astype(BF16)
        queries = [head_stack(query[:, g * GROUP : (g + 1) * GROUP]) for g in range(groups)]

        units = [(i, g) for i in range(images) for g in range(groups)]

        def places(i, g):
            return (
                slice(i * patches, (i + 1) * patches),
                slice(g * GROUP, (g + 1) * GROUP),
                slice(g * stacked, (g + 1) * stacked),
            )

        def score(i, g):
            at, cols, _ = places(i, g)
            return dot_t(keys[at, cols], queries[g])

        pooled = [[] for _ in range(images)]
        inverse = [[] for _ in range(images)]
        ahead = score(*units[0])
        for n, (i, g) in enumerate(units):
            at, cols, to = places(i, g)
            scores = ahead
            if n + 1 < len(units):
                ahead = score(*units[n + 1])
            if n < len(before):
                before[n]()
            scores = jnp.exp(scores - jnp.max(scores, axis=0, keepdims=True))
            inverse[i].append(1.0 / jnp.sum(scores, axis=0, keepdims=True))
            weights = scores.astype(BF16)
            weights_ref[which, at, to] = weights
            pooled[i].append(head_blocks(dot(values_t[cols, at], weights) * inverse[i][g], block))
        pooled = [jnp.concatenate(found, axis=0).T.astype(BF16) for found in pooled]
        mixed = dot(jnp.concatenate(pooled, axis=0), wo[...])
        caption_2 = jnp.concatenate([caption] * images, axis=0)
        owner_2 = jnp.concatenate([owner] * images, axis=0)
        image = (
            lax.broadcasted_iota(jnp.int32, (images * block, 1), 0) // block + me * images
        ).astype(F32)
        inner = jnp.sum(mixed * caption_2, axis=1, keepdims=True)
        mixed_inv = lax.rsqrt(jnp.sum(mixed * mixed, axis=1, keepdims=True) + NORM_EPS)
        caption_inv = lax.rsqrt(jnp.sum(caption * caption, axis=1, keepdims=True) + NORM_EPS)
        caption_inv = jnp.concatenate([caption_inv] * images, axis=0)
        cosine = inner * mixed_inv * caption_inv
        logit = LOGIT_SCALE * cosine + LOGIT_BIAS
        label = jnp.where(owner_2 == image, 1.0, -1.0)
        slope = -LOGIT_SCALE * label / (1.0 + jnp.exp(label * logit))
        across = slope * mixed_inv * caption_inv
        grad_mixed = across * caption_2 - (slope * cosine * mixed_inv * mixed_inv) * mixed
        by_caption = jnp.concatenate([head_columns(rows_, block) for rows_ in inverse], axis=0)
        grad_pooled = (dot_t(grad_mixed.astype(BF16), wo[...]) * by_caption).astype(BF16)
        if own:
            direct = across * mixed - (slope * cosine * caption_inv * caption_inv) * caption_2
            direct = sum(direct[i * block : (i + 1) * block] for i in range(images))

        def grad_weight(i, g):
            at, cols, _ = places(i, g)
            grads = head_stack(grad_pooled[i * block : (i + 1) * block, cols])
            return grads, dot_t(values[at, cols], grads)

        grad_query = [None] * groups
        ahead = grad_weight(*units[0])
        for n, (i, g) in enumerate(units):
            at, cols, to = places(i, g)
            grads, grad_weights = ahead
            if n + 1 < len(units):
                ahead = grad_weight(*units[n + 1])
            weights = weights_ref[which, at, to].astype(F32)
            mean = jnp.sum(weights * grad_weights, axis=0, keepdims=True) * inverse[i][g]
            grad_scores = (weights * (grad_weights - mean)).astype(BF16)
            later.append(
                functools.partial(finish, at, cols, to, grads, grad_scores, queries[g], which)
            )
            if own:
                found = head_blocks(dot(keys_t[cols, at], grad_scores), block)
                grad_query[g] = found if grad_query[g] is None else grad_query[g] + found
            else:
                later.pop()()
        if own:
            grad_query = jnp.concatenate(grad_query, axis=0).T * HEAD_DIM**-0.5
            grad = direct + dot_t(grad_query.astype(BF16), wq[...])
            grad = grad.reshape(slots, rows, d)
            part[pl.ds(slot, slots)] = jnp.concatenate(
                [grad[:, :, :half], grad[:, :, half:]], axis=1
            ).astype(BF16)
        return later

    def finish(at, cols, to, grads, grad_scores, queries, which):
        add(gv, gv_out, at, cols, dot(weights_ref[which, at, to], grads), which)
        add(gk, gk_out, at, cols, dot(grad_scores, queries), which)

    def run_all(which, own, before=()):
        if blocks == 1:
            return run_block(0, which, own, before)

        @pl.loop(0, blocks)
        def _(n):
            for work in run_block(n * slots, which, own):
                work()

        return []

    later = run_all(0, True)

    @pl.loop(1, nb, unroll=unroll)
    def _(step):
        part_copy(step).start()

    for step in range(1, ns):
        span_copy(step, step).wait_recv()
        span_owner_copy(step, step).wait_recv()
        later = run_all(step, False, later)
    for work in later:
        work()
    if blocks > 1:
        gk_out[...] = gk[...].astype(BF16)
        gv_out[...] = gv[...].astype(BF16)

    all_parts.wait_recv()

    parts_in[me] = part[me]
    sum_out[...] = jnp.sum(parts_in[...].astype(F32), axis=0)

    all_caps.wait_send()
    all_owners.wait_send()
    all_parts.wait_send()

    for step in range(1, ns):
        span_copy(step, ns - step).wait_send()
        span_owner_copy(step, ns - step).wait_send()


def token_kernel(patches, sum_ref, gk, gv, wk, wv, caption_out, token_out, unfolded, made, sems):
    rows, d = caption_out.shape
    summed = sum_ref[...] * CAPTION_SCALE
    unfolded[...] = jnp.concatenate([summed[:rows], summed[rows:]], axis=1)
    copies = [pltpu.make_async_copy(unfolded, caption_out, sems.at[0])]
    copies[0].start()
    for n in range(d // GROUP):
        at = pl.ds(n * GROUP, GROUP)
        made[:, at] = patches * (dot_t(gk[...], wk[at, :]) + dot_t(gv[...], wv[at, :]))
        copies.append(pltpu.make_async_copy(made.at[:, at], token_out.at[:, at], sems.at[n + 1]))
        copies[-1].start()
    for copy in copies:
        copy.wait()


def hold(x):
    return pltpu.with_memory_space_constraint(x, pltpu.HBM)


def on_device(nb, ns, image_tokens, captions, owner, w_query, w_key, w_value, w_out):
    images, patches, d = image_tokens.shape
    rows = captions.shape[0]
    total = images * patches
    block = math.gcd(nb * rows, LANES)
    vmem = pl.BlockSpec(memory_space=pltpu.VMEM)
    hbm = pl.BlockSpec(memory_space=pltpu.HBM)
    heads = d // HEAD_DIM
    dma = pltpu.SemaphoreType.DMA
    gk, gv, summed, wk, wv = pl.pallas_call(
        functools.partial(pair_kernel, nb, ns, images),
        out_shape=(
            jax.ShapeDtypeStruct((total, d), BF16),
            jax.ShapeDtypeStruct((total, d), BF16),
            jax.ShapeDtypeStruct((2 * rows, d // 2), F32),
            jax.ShapeDtypeStruct((d, d), BF16),
            jax.ShapeDtypeStruct((d, d), BF16),
        ),
        in_specs=[hbm] * 7,
        out_specs=(vmem,) * 5,
        scratch_shapes=[
            pltpu.VMEM((rows, d), BF16),
            pltpu.VMEM((1, rows), jnp.int32),
            pltpu.VMEM((total, d), BF16),
            pltpu.VMEM((d, d), BF16),
            pltpu.VMEM((d, d), BF16),
            pltpu.VMEM((total, d), BF16),
            pltpu.VMEM((total, d), BF16),
            pltpu.VMEM((d, total), BF16),
            pltpu.VMEM((d, total), BF16),
            pltpu.VMEM((ns, total, heads * block), BF16),
            pltpu.VMEM((total, d), F32),
            pltpu.VMEM((total, d), F32),
            pltpu.VMEM((ns, nb, 2 * rows, d // 2), BF16),
            pltpu.VMEM((ns, nb, 1, LANES), jnp.int32),
            pltpu.VMEM((nb, 2 * rows, d // 2), BF16),
            pltpu.VMEM((nb, 2 * rows, d // 2), BF16),
            dma((7,)),
            dma,
            dma,
            dma,
            dma,
            dma((ns,)),
            dma((ns,)),
            dma((ns,)),
            dma((ns,)),
            dma,
            dma,
        ],
        compiler_params=pltpu.CompilerParams(
            collective_id=0, has_side_effects=True, vmem_limit_bytes=36 * 2**20
        ),
        name="pairs",
    )(
        hold(captions),
        hold(owner.reshape(1, rows)),
        hold(image_tokens.reshape(total, d)),
        hold(w_query),
        hold(w_key),
        hold(w_value),
        hold(w_out),
    )
    caption_grad, token_grad = pl.pallas_call(
        functools.partial(token_kernel, patches),
        out_shape=(
            jax.ShapeDtypeStruct((rows, d), F32),
            jax.ShapeDtypeStruct((total, d), F32),
        ),
        in_specs=[vmem] * 5,
        out_specs=(hbm, hbm),
        scratch_shapes=[
            pltpu.VMEM((rows, d), F32),
            pltpu.VMEM((total, d), F32),
            dma((d // GROUP + 1,)),
        ],
        compiler_params=pltpu.CompilerParams(vmem_limit_bytes=16 * 2**20),
        name="token_grad",
    )(summed, gk, gv, wk, wv)
    return (caption_grad, token_grad.reshape(images, patches, d))


def solution(mesh):
    placed = (
        P("batch", None, None),
        P(("batch", "span"), None),
        P(("batch", "span")),
        P(),
        P(),
        P(),
        P(),
    )
    return jax.shard_map(
        functools.partial(on_device, mesh.shape["batch"], mesh.shape["span"]),
        mesh=mesh,
        in_specs=placed,
        out_specs=(P(("batch", "span"), None), P("batch", None, None)),
        check_vma=False,
    )
```

```python
import functools
import math

import jax
import jax.numpy as jnp
from jax import lax
from jax.experimental import pallas as pl
from jax.experimental.pallas import tpu as pltpu
from jax.sharding import PartitionSpec as P

HEAD_DIM = 64
LOGIT_SCALE = 10.0
LOGIT_BIAS = -2.0
NORM_EPS = 1e-06
CAPTION_SCALE = 16.0
LANES = 128
GROUP = 256
HEADS_IN_GROUP = GROUP // HEAD_DIM
F32 = jnp.float32
BF16 = jnp.bfloat16
MESH = pl.DeviceIdType.MESH


def dot(a, b):
    return jnp.dot(a, b, preferred_element_type=F32)


def dot_t(a, b):
    return lax.dot_general(a, b, (((1,), (1,)), ((), ())), preferred_element_type=F32)


def head_masks(tile):
    head = lax.broadcasted_iota(jnp.int32, (tile, GROUP), 1) // HEAD_DIM
    return [(head == h).astype(F32).astype(BF16) for h in range(HEADS_IN_GROUP)]


def head_stack(x):
    tile = math.gcd(x.shape[0], 16)
    tiles = x.reshape(x.shape[0] // tile, tile, GROUP)
    return jnp.concatenate([(tiles * m).reshape(x.shape) for m in head_masks(tile)], axis=0)


def head_blocks(x, width):
    return jnp.concatenate(
        [
            x[h * HEAD_DIM : (h + 1) * HEAD_DIM, h * width : (h + 1) * width]
            for h in range(HEADS_IN_GROUP)
        ],
        axis=0,
    )


def by_head(rows, width):
    return [rows[:, h * width : (h + 1) * width] for h in range(HEADS_IN_GROUP)]


def pair_kernel(
    nb,
    ns,
    images,
    captions_hbm,
    owner_hbm,
    tokens_hbm,
    wq_hbm,
    wk_hbm,
    wv_hbm,
    wo_hbm,
    token_out,
    sum_out,
    captions_ref,
    owner_ref,
    tokens,
    wq,
    wk,
    wv,
    wo,
    keys,
    values,
    keys_t,
    values_t,
    weights_ref,
    gk,
    gv,
    gk_b,
    gv_b,
    caps,
    owners,
    part,
    parts_in,
    load_sem,
    cap_send,
    cap_recv,
    owner_send,
    owner_recv,
    span_send,
    span_recv,
    span_owner_send,
    span_owner_recv,
    part_send,
    part_recv,
):
    me = lax.axis_index("batch")
    my_span = lax.axis_index("span")
    rows = captions_ref.shape[0]
    d = captions_ref.shape[1]
    half = d // 2
    patches = tokens.shape[0] // images
    groups = d // GROUP
    block = math.gcd(nb * rows, LANES)
    slots = block // rows
    blocks = nb * rows // block
    stacked = HEADS_IN_GROUP * block
    unroll = nb <= 16

    def peer_of(step):
        return lax.rem(me + step, nb)

    def span_of(step):
        return lax.rem(my_span + step, ns)

    loads = [
        pltpu.make_async_copy(src, dst, load_sem.at[n])
        for n, (src, dst) in enumerate(
            (
                (captions_hbm, captions_ref),
                (owner_hbm, owner_ref),
                (tokens_hbm, tokens),
                (wk_hbm, wk),
                (wv_hbm, wv),
                (wq_hbm, wq),
                (wo_hbm, wo),
            )
        )
    ]
    for load in loads[:2]:
        load.start()

    barrier = pltpu.get_barrier_semaphore()

    @pl.loop(1, nb, unroll=unroll)
    def _(step):
        pl.semaphore_signal(
            barrier, inc=1, device_id={"batch": peer_of(step)}, device_id_type=MESH
        )

    for step in range(1, ns):
        pl.semaphore_signal(
            barrier, inc=1, device_id={"span": span_of(step)}, device_id_type=MESH
        )

    for load in loads[2:]:
        load.start()
    for load in loads[:2]:
        load.wait()
    mine = captions_ref[...].astype(F32)
    caps[0, me] = jnp.concatenate([mine[:, :half], mine[:, half:]], axis=0).astype(BF16)
    owners[0, me] = jnp.concatenate(
        [owner_ref[...], jnp.zeros((1, LANES - rows), jnp.int32)], axis=1
    )

    pl.semaphore_wait(barrier, nb + ns - 2)

    def cap_copy(step):
        return pltpu.make_async_remote_copy(
            src_ref=caps.at[0, me],
            dst_ref=caps.at[0, me],
            send_sem=cap_send,
            recv_sem=cap_recv,
            device_id={"batch": peer_of(step)},
            device_id_type=MESH,
        )

    def owner_copy(step):
        return pltpu.make_async_remote_copy(
            src_ref=owners.at[0, me],
            dst_ref=owners.at[0, me],
            send_sem=owner_send,
            recv_sem=owner_recv,
            device_id={"batch": peer_of(step)},
            device_id_type=MESH,
        )

    def part_copy(step):
        return pltpu.make_async_remote_copy(
            src_ref=part.at[peer_of(step)],
            dst_ref=parts_in.at[me],
            send_sem=part_send,
            recv_sem=part_recv,
            device_id={"batch": peer_of(step)},
            device_id_type=MESH,
        )

    def span_copy(step, slot):
        return pltpu.make_async_remote_copy(
            src_ref=caps.at[0],
            dst_ref=caps.at[ns - step],
            send_sem=span_send.at[step],
            recv_sem=span_recv.at[slot],
            device_id={"span": span_of(step)},
            device_id_type=MESH,
        )

    def whole(ref, send_sem, recv_sem):
        return pltpu.make_async_remote_copy(
            src_ref=ref.at[pl.ds(0, nb - 1)],
            dst_ref=ref.at[pl.ds(0, nb - 1)],
            send_sem=send_sem,
            recv_sem=recv_sem,
            device_id={"batch": peer_of(1)},
            device_id_type=MESH,
        )

    all_caps = whole(caps.at[0], cap_send, cap_recv)
    all_owners = whole(owners.at[0], owner_send, owner_recv)
    all_parts = whole(parts_in, part_send, part_recv)

    def span_owner_copy(step, slot):
        return pltpu.make_async_remote_copy(
            src_ref=owners.at[0],
            dst_ref=owners.at[ns - step],
            send_sem=span_owner_send.at[step],
            recv_sem=span_owner_recv.at[slot],
            device_id={"span": span_of(step)},
            device_id_type=MESH,
        )

    @pl.loop(1, nb, unroll=unroll)
    def _(step):
        cap_copy(step).start()

    @pl.loop(1, nb, unroll=unroll)
    def _(step):
        owner_copy(step).start()

    for load in loads[2:5]:
        load.wait()
    for i in range(images):
        at = pl.ds(i * patches, patches)
        found = dot(tokens[at, :], wk[...])
        keys[at, :] = found.astype(BF16)
        keys_t[:, at] = found.astype(BF16).T
        found = dot(tokens[at, :], wv[...])
        values[at, :] = found.astype(BF16)
        values_t[:, at] = found.astype(BF16).T
    if blocks > 1:
        gk[...] = jnp.zeros_like(gk)
        gv[...] = jnp.zeros_like(gv)
    for load in loads[5:]:
        load.wait()

    all_caps.wait_recv()

    for step in range(1, ns):
        span_copy(step, ns - step).start()

    all_owners.wait_recv()

    for step in range(1, ns):
        span_owner_copy(step, ns - step).start()

    def add(total, out, at, cols, found, which):
        if blocks > 1 or which > 0:
            found = total[at, cols] + found
        if blocks == 1 and which == ns - 1:
            out[at, cols] = found.astype(BF16)
        else:
            total[at, cols] = found

    def run_block(slot, which, own, before=()):
        later = []
        held = caps[which, pl.ds(slot, slots)].astype(F32)
        caption = jnp.concatenate(
            [
                held[:, :rows].reshape(block, half),
                held[:, rows:].reshape(block, half),
            ],
            axis=1,
        )
        owner = owners[which, pl.ds(slot, slots)]
        owner = jnp.broadcast_to(owner, (slots, rows, LANES))
        row = lax.broadcasted_iota(jnp.int32, owner.shape, 1)
        lane = lax.broadcasted_iota(jnp.int32, owner.shape, 2)
        owner = jnp.sum(
            jnp.where(row == lane, owner, 0).astype(F32).reshape(block, LANES),
            axis=1,
            keepdims=True,
        )
        query = (dot(caption.astype(BF16), wq[...]) * HEAD_DIM**-0.5).astype(BF16)
        queries = [head_stack(query[:, g * GROUP : (g + 1) * GROUP]) for g in range(groups)]

        units = [(i, g) for i in range(images) for g in range(groups)]

        def places(i, g):
            return (
                slice(i * patches, (i + 1) * patches),
                slice(g * GROUP, (g + 1) * GROUP),
                slice(g * stacked, (g + 1) * stacked),
            )

        def score(i, g):
            at, cols, _ = places(i, g)
            return dot_t(keys[at, cols], queries[g])

        pooled = [[] for _ in range(images)]
        inverse = [[] for _ in range(images)]
        ahead = score(*units[0])
        for n, (i, g) in enumerate(units):
            at, cols, to = places(i, g)
            scores = ahead
            if n + 1 < len(units):
                ahead = score(*units[n + 1])
            if n < len(before):
                before[n]()
            scores = jnp.exp(scores - jnp.max(scores, axis=0, keepdims=True))
            inverse[i].append(1.0 / jnp.sum(scores, axis=0, keepdims=True))
            weights = scores.astype(BF16)
            weights_ref[which, at, to] = weights
            pooled[i].append(head_blocks(dot(values_t[cols, at], weights) * inverse[i][g], block))
        pooled_t = pooled
        pooled = [jnp.concatenate(found, axis=0).T.astype(BF16) for found in pooled]
        mixed = dot(jnp.concatenate(pooled, axis=0), wo[...])
        caption_2 = jnp.concatenate([caption] * images, axis=0)
        owner_2 = jnp.concatenate([owner] * images, axis=0)
        image = (
            lax.broadcasted_iota(jnp.int32, (images * block, 1), 0) // block + me * images
        ).astype(F32)
        inner = jnp.sum(mixed * caption_2, axis=1, keepdims=True)
        mixed_inv = lax.rsqrt(jnp.sum(mixed * mixed, axis=1, keepdims=True) + NORM_EPS)
        caption_inv = lax.rsqrt(jnp.sum(caption * caption, axis=1, keepdims=True) + NORM_EPS)
        caption_inv = jnp.concatenate([caption_inv] * images, axis=0)
        cosine = inner * mixed_inv * caption_inv
        logit = LOGIT_SCALE * cosine + LOGIT_BIAS
        label = jnp.where(owner_2 == image, 1.0, -1.0)
        slope = -LOGIT_SCALE * label / (1.0 + jnp.exp(label * logit))
        across = slope * mixed_inv * caption_inv
        grad_mixed = across * caption_2 - (slope * cosine * mixed_inv * mixed_inv) * mixed
        grad_pooled_t = dot_t(wo[...], grad_mixed.astype(BF16))
        if own:
            direct = across * mixed - (slope * cosine * caption_inv * caption_inv) * caption_2
            direct = sum(direct[i * block : (i + 1) * block] for i in range(images))

        grad_pooled = []
        means = []
        for i in range(images):
            scale = jnp.concatenate(
                [
                    jnp.broadcast_to(row, (HEAD_DIM, block))
                    for rows_ in inverse[i]
                    for row in by_head(rows_, block)
                ],
                axis=0,
            )
            found = (grad_pooled_t[:, i * block : (i + 1) * block] * scale).astype(BF16)
            grad_pooled.append(found.T)
            products = found.astype(F32) * jnp.concatenate(pooled_t[i], axis=0)
            products = [
                jnp.sum(products[h * HEAD_DIM : (h + 1) * HEAD_DIM], axis=0, keepdims=True)
                for h in range(d // HEAD_DIM)
            ]
            means.append(
                [
                    jnp.concatenate(
                        products[g * HEADS_IN_GROUP : (g + 1) * HEADS_IN_GROUP], axis=1
                    )
                    for g in range(groups)
                ]
            )

        def grad_weight(i, g):
            at, cols, _ = places(i, g)
            grads = head_stack(grad_pooled[i][:, cols])
            return grads, dot_t(values[at, cols], grads)

        grad_query = [None] * groups
        ahead = grad_weight(*units[0])
        for n, (i, g) in enumerate(units):
            at, cols, to = places(i, g)
            grads, grad_weights = ahead
            if n + 1 < len(units):
                ahead = grad_weight(*units[n + 1])
            weights = weights_ref[which, at, to].astype(F32)
            grad_scores = (weights * (grad_weights - means[i][g])).astype(BF16)
            later.append(
                functools.partial(finish, at, cols, to, grads, grad_scores, queries[g], which)
            )
            if own:
                found = head_blocks(dot(keys_t[cols, at], grad_scores), block)
                grad_query[g] = found if grad_query[g] is None else grad_query[g] + found
            else:
                later.pop()()
                if blocks == 1 and which == ns - 1 and g == groups - 1:
                    token_product(at)
        if own:
            grad_query = jnp.concatenate(grad_query, axis=0).T * HEAD_DIM**-0.5
            grad = direct + dot_t(grad_query.astype(BF16), wq[...])
            grad = grad.reshape(slots, rows, d)
            part[pl.ds(slot, slots)] = jnp.concatenate(
                [grad[:, :, :half], grad[:, :, half:]], axis=1
            ).astype(BF16)
        return later

    def token_product(at):
        token_out[at, :] = patches * (dot_t(gk_b[at, :], wk[...]) + dot_t(gv_b[at, :], wv[...]))

    def finish(at, cols, to, grads, grad_scores, queries, which):
        add(gv, gv_b, at, cols, dot(weights_ref[which, at, to], grads), which)
        add(gk, gk_b, at, cols, dot(grad_scores, queries), which)

    def run_all(which, own, before=()):
        if blocks == 1:
            return run_block(0, which, own, before)

        @pl.loop(0, blocks)
        def _(n):
            for work in run_block(n * slots, which, own):
                work()

        return []

    later = run_all(0, True)

    @pl.loop(1, nb, unroll=unroll)
    def _(step):
        part_copy(step).start()

    for step in range(1, ns):
        span_copy(step, step).wait_recv()
        span_owner_copy(step, step).wait_recv()
        later = run_all(step, False, later)
    for work in later:
        work()
    if blocks > 1:
        gk_b[...] = gk[...].astype(BF16)
        gv_b[...] = gv[...].astype(BF16)
    if blocks > 1 or ns == 1:
        for i in range(images):
            token_product(slice(i * patches, (i + 1) * patches))

    all_parts.wait_recv()

    parts_in[me] = part[me]
    sum_out[...] = jnp.sum(parts_in[...].astype(F32), axis=0)

    all_caps.wait_send()
    all_owners.wait_send()
    all_parts.wait_send()

    for step in range(1, ns):
        span_copy(step, ns - step).wait_send()
        span_owner_copy(step, ns - step).wait_send()


def write_kernel(sum_ref, token_ref, caption_out, token_out, unfolded, sems):
    rows, d = caption_out.shape
    count = sems.shape[0] - 1
    chunk = token_ref.shape[0] // count
    copies = [
        pltpu.make_async_copy(
            token_ref.at[pl.ds(n * chunk, chunk)],
            token_out.at[pl.ds(n * chunk, chunk)],
            sems.at[n],
        )
        for n in range(count)
    ]
    for copy in copies:
        copy.start()
    summed = sum_ref[...] * CAPTION_SCALE
    unfolded[...] = jnp.concatenate([summed[:rows], summed[rows:]], axis=1)
    copies.append(pltpu.make_async_copy(unfolded, caption_out, sems.at[count]))
    copies[-1].start()
    for copy in copies:
        copy.wait()


def hold(x):
    return pltpu.with_memory_space_constraint(x, pltpu.HBM)


def on_device(nb, ns, image_tokens, captions, owner, w_query, w_key, w_value, w_out):
    images, patches, d = image_tokens.shape
    rows = captions.shape[0]
    total = images * patches
    block = math.gcd(nb * rows, LANES)
    vmem = pl.BlockSpec(memory_space=pltpu.VMEM)
    hbm = pl.BlockSpec(memory_space=pltpu.HBM)
    heads = d // HEAD_DIM
    dma = pltpu.SemaphoreType.DMA
    token_terms, summed = pl.pallas_call(
        functools.partial(pair_kernel, nb, ns, images),
        out_shape=(
            jax.ShapeDtypeStruct((total, d), F32),
            jax.ShapeDtypeStruct((2 * rows, d // 2), F32),
        ),
        in_specs=[hbm] * 7,
        out_specs=(vmem, vmem),
        scratch_shapes=[
            pltpu.VMEM((rows, d), BF16),
            pltpu.VMEM((1, rows), jnp.int32),
            pltpu.VMEM((total, d), BF16),
            pltpu.VMEM((d, d), BF16),
            pltpu.VMEM((d, d), BF16),
            pltpu.VMEM((d, d), BF16),
            pltpu.VMEM((d, d), BF16),
            pltpu.VMEM((total, d), BF16),
            pltpu.VMEM((total, d), BF16),
            pltpu.VMEM((d, total), BF16),
            pltpu.VMEM((d, total), BF16),
            pltpu.VMEM((ns, total, heads * block), BF16),
            pltpu.VMEM((total, d), F32),
            pltpu.VMEM((total, d), F32),
            pltpu.VMEM((total, d), BF16),
            pltpu.VMEM((total, d), BF16),
            pltpu.VMEM((ns, nb, 2 * rows, d // 2), BF16),
            pltpu.VMEM((ns, nb, 1, LANES), jnp.int32),
            pltpu.VMEM((nb, 2 * rows, d // 2), BF16),
            pltpu.VMEM((nb, 2 * rows, d // 2), BF16),
            dma((7,)),
            dma,
            dma,
            dma,
            dma,
            dma((ns,)),
            dma((ns,)),
            dma((ns,)),
            dma((ns,)),
            dma,
            dma,
        ],
        compiler_params=pltpu.CompilerParams(
            collective_id=0, has_side_effects=True, vmem_limit_bytes=36 * 2**20
        ),
        name="pairs",
    )(
        hold(captions),
        hold(owner.reshape(1, rows)),
        hold(image_tokens.reshape(total, d)),
        hold(w_query),
        hold(w_key),
        hold(w_value),
        hold(w_out),
    )
    caption_grad, token_grad = pl.pallas_call(
        write_kernel,
        out_shape=(
            jax.ShapeDtypeStruct((rows, d), F32),
            jax.ShapeDtypeStruct((total, d), F32),
        ),
        in_specs=[vmem, vmem],
        out_specs=(hbm, hbm),
        scratch_shapes=[
            pltpu.VMEM((rows, d), F32),
            dma((2 * images + 1,)),
        ],
        compiler_params=pltpu.CompilerParams(vmem_limit_bytes=16 * 2**20),
        name="write",
    )(summed, token_terms)
    return (caption_grad, token_grad.reshape(images, patches, d))


def solution(mesh):
    placed = (
        P("batch", None, None),
        P(("batch", "span"), None),
        P(("batch", "span")),
        P(),
        P(),
        P(),
        P(),
    )
    return jax.shard_map(
        functools.partial(on_device, mesh.shape["batch"], mesh.shape["span"]),
        mesh=mesh,
        in_specs=placed,
        out_specs=(P(("batch", "span"), None), P("batch", None, None)),
        check_vma=False,
    )
```

```python
import functools
import math

import jax
import jax.numpy as jnp
from jax import lax
from jax.experimental import pallas as pl
from jax.experimental.pallas import tpu as pltpu
from jax.sharding import PartitionSpec as P

HEAD_DIM = 64
LOGIT_SCALE = 10.0
LOGIT_BIAS = -2.0
NORM_EPS = 1e-06
CAPTION_SCALE = 16.0
LANES = 128
GROUP = 256
HEADS_IN_GROUP = GROUP // HEAD_DIM
F32 = jnp.float32
BF16 = jnp.bfloat16
MESH = pl.DeviceIdType.MESH


def dot(a, b):
    return jnp.dot(a, b, preferred_element_type=F32)


def dot_t(a, b):
    return lax.dot_general(a, b, (((1,), (1,)), ((), ())), preferred_element_type=F32)


def head_masks(tile):
    head = lax.broadcasted_iota(jnp.int32, (tile, GROUP), 1) // HEAD_DIM
    return [(head == h).astype(F32).astype(BF16) for h in range(HEADS_IN_GROUP)]


def head_stack(x):
    tile = math.gcd(x.shape[0], 16)
    tiles = x.reshape(x.shape[0] // tile, tile, GROUP)
    return jnp.concatenate([(tiles * m).reshape(x.shape) for m in head_masks(tile)], axis=0)


def head_blocks(x, width):
    return jnp.concatenate(
        [
            x[h * HEAD_DIM : (h + 1) * HEAD_DIM, h * width : (h + 1) * width]
            for h in range(HEADS_IN_GROUP)
        ],
        axis=0,
    )


def by_head(rows, width):
    return [rows[:, h * width : (h + 1) * width] for h in range(HEADS_IN_GROUP)]


def pair_kernel(
    nb,
    ns,
    images,
    captions_hbm,
    owner_hbm,
    tokens_hbm,
    wq_hbm,
    wk_hbm,
    wv_hbm,
    wo_hbm,
    token_out,
    sum_out,
    captions_ref,
    owner_ref,
    tokens,
    wq,
    wk,
    wv,
    wo,
    keys,
    values,
    keys_t,
    values_t,
    weights_ref,
    gk,
    gv,
    gk_b,
    gv_b,
    caps,
    owners,
    part,
    parts_in,
    load_sem,
    cap_send,
    cap_recv,
    owner_send,
    owner_recv,
    span_send,
    span_recv,
    span_owner_send,
    span_owner_recv,
    part_send,
    part_recv,
):
    me = lax.axis_index("batch")
    my_span = lax.axis_index("span")
    rows = captions_ref.shape[0]
    d = captions_ref.shape[1]
    half = d // 2
    patches = tokens.shape[0] // images
    groups = d // GROUP
    block = math.gcd(nb * rows, LANES)
    slots = block // rows
    blocks = nb * rows // block
    stacked = HEADS_IN_GROUP * block
    unroll = nb <= 16

    def peer_of(step):
        return lax.rem(me + step, nb)

    def span_of(step):
        return lax.rem(my_span + step, ns)

    loads = [
        pltpu.make_async_copy(src, dst, load_sem.at[n])
        for n, (src, dst) in enumerate(
            (
                (captions_hbm, captions_ref),
                (owner_hbm, owner_ref),
                (tokens_hbm, tokens),
                (wk_hbm, wk),
                (wv_hbm, wv),
                (wq_hbm, wq),
                (wo_hbm, wo),
            )
        )
    ]
    for load in loads[:2]:
        load.start()

    barrier = pltpu.get_barrier_semaphore()

    @pl.loop(1, nb, unroll=unroll)
    def _(step):
        pl.semaphore_signal(
            barrier, inc=1, device_id={"batch": peer_of(step)}, device_id_type=MESH
        )

    for step in range(1, ns):
        pl.semaphore_signal(
            barrier, inc=1, device_id={"span": span_of(step)}, device_id_type=MESH
        )

    for load in loads[2:]:
        load.start()
    for load in loads[:2]:
        load.wait()
    mine = captions_ref[...].astype(F32)
    caps[0, me] = jnp.concatenate([mine[:, :half], mine[:, half:]], axis=0).astype(BF16)
    owners[0, me] = jnp.concatenate(
        [owner_ref[...], jnp.zeros((1, LANES - rows), jnp.int32)], axis=1
    )

    pl.semaphore_wait(barrier, nb + ns - 2)

    def cap_copy(step):
        return pltpu.make_async_remote_copy(
            src_ref=caps.at[0, me],
            dst_ref=caps.at[0, me],
            send_sem=cap_send,
            recv_sem=cap_recv,
            device_id={"batch": peer_of(step)},
            device_id_type=MESH,
        )

    def owner_copy(step):
        return pltpu.make_async_remote_copy(
            src_ref=owners.at[0, me],
            dst_ref=owners.at[0, me],
            send_sem=owner_send,
            recv_sem=owner_recv,
            device_id={"batch": peer_of(step)},
            device_id_type=MESH,
        )

    def part_copy(step):
        return pltpu.make_async_remote_copy(
            src_ref=part.at[peer_of(step)],
            dst_ref=parts_in.at[me],
            send_sem=part_send,
            recv_sem=part_recv,
            device_id={"batch": peer_of(step)},
            device_id_type=MESH,
        )

    def span_copy(step, slot):
        return pltpu.make_async_remote_copy(
            src_ref=caps.at[0],
            dst_ref=caps.at[ns - step],
            send_sem=span_send.at[step],
            recv_sem=span_recv.at[slot],
            device_id={"span": span_of(step)},
            device_id_type=MESH,
        )

    def whole(ref, send_sem, recv_sem):
        return pltpu.make_async_remote_copy(
            src_ref=ref.at[pl.ds(0, nb - 1)],
            dst_ref=ref.at[pl.ds(0, nb - 1)],
            send_sem=send_sem,
            recv_sem=recv_sem,
            device_id={"batch": peer_of(1)},
            device_id_type=MESH,
        )

    all_caps = whole(caps.at[0], cap_send, cap_recv)
    all_owners = whole(owners.at[0], owner_send, owner_recv)
    all_parts = whole(parts_in, part_send, part_recv)

    def span_owner_copy(step, slot):
        return pltpu.make_async_remote_copy(
            src_ref=owners.at[0],
            dst_ref=owners.at[ns - step],
            send_sem=span_owner_send.at[step],
            recv_sem=span_owner_recv.at[slot],
            device_id={"span": span_of(step)},
            device_id_type=MESH,
        )

    @pl.loop(1, nb, unroll=unroll)
    def _(step):
        cap_copy(step).start()

    @pl.loop(1, nb, unroll=unroll)
    def _(step):
        owner_copy(step).start()

    for load in loads[2:5]:
        load.wait()
    found = dot(tokens[...], wk[...]).astype(BF16)
    keys[...] = found
    keys_t[...] = found.T
    found = dot(tokens[...], wv[...]).astype(BF16)
    values[...] = found
    values_t[...] = found.T
    if blocks > 1:
        gk[...] = jnp.zeros_like(gk)
        gv[...] = jnp.zeros_like(gv)
    for load in loads[5:]:
        load.wait()

    all_caps.wait_recv()

    for step in range(1, ns):
        span_copy(step, ns - step).start()

    all_owners.wait_recv()

    for step in range(1, ns):
        span_owner_copy(step, ns - step).start()

    def add(total, out, at, cols, found, which):
        if blocks > 1 or which > 0:
            found = total[at, cols] + found
        if blocks == 1 and which == ns - 1:
            out[at, cols] = found.astype(BF16)
        else:
            total[at, cols] = found

    def run_block(slot, which, own, before=()):
        later = []
        held = caps[which, pl.ds(slot, slots)].astype(F32)
        caption = jnp.concatenate(
            [
                held[:, :rows].reshape(block, half),
                held[:, rows:].reshape(block, half),
            ],
            axis=1,
        )
        owner = owners[which, pl.ds(slot, slots)]
        owner = jnp.broadcast_to(owner, (slots, rows, LANES))
        row = lax.broadcasted_iota(jnp.int32, owner.shape, 1)
        lane = lax.broadcasted_iota(jnp.int32, owner.shape, 2)
        owner = jnp.sum(
            jnp.where(row == lane, owner, 0).astype(F32).reshape(block, LANES),
            axis=1,
            keepdims=True,
        )
        query = (dot(caption.astype(BF16), wq[...]) * HEAD_DIM**-0.5).astype(BF16)
        queries = [head_stack(query[:, g * GROUP : (g + 1) * GROUP]) for g in range(groups)]

        units = [(i, g) for g in range(groups) for i in range(images)]

        def places(i, g):
            return (
                slice(i * patches, (i + 1) * patches),
                slice(g * GROUP, (g + 1) * GROUP),
                slice(g * stacked, (g + 1) * stacked),
            )

        def score(g):
            return dot_t(keys[:, g * GROUP : (g + 1) * GROUP], queries[g])

        pooled = [[] for _ in range(images)]
        inverse = [[] for _ in range(images)]
        both = score(0)
        for n, (i, g) in enumerate(units):
            at, cols, to = places(i, g)
            scores = both[at]
            if i + 1 == images and g + 1 < groups:
                both = score(g + 1)
            for work in before[n :: len(units)]:
                work()
            scores = jnp.exp(scores - jnp.max(scores, axis=0, keepdims=True))
            inverse[i].append(1.0 / jnp.sum(scores, axis=0, keepdims=True))
            weights = scores.astype(BF16)
            weights_ref[which, at, to] = weights
            pooled[i].append(head_blocks(dot(values_t[cols, at], weights) * inverse[i][g], block))
        pooled_t = pooled
        pooled = [jnp.concatenate(found, axis=0).T.astype(BF16) for found in pooled]
        mixed = dot(jnp.concatenate(pooled, axis=0), wo[...])
        caption_2 = jnp.concatenate([caption] * images, axis=0)
        owner_2 = jnp.concatenate([owner] * images, axis=0)
        image = (
            lax.broadcasted_iota(jnp.int32, (images * block, 1), 0) // block + me * images
        ).astype(F32)
        inner = jnp.sum(mixed * caption_2, axis=1, keepdims=True)
        mixed_inv = lax.rsqrt(jnp.sum(mixed * mixed, axis=1, keepdims=True) + NORM_EPS)
        caption_inv = lax.rsqrt(jnp.sum(caption * caption, axis=1, keepdims=True) + NORM_EPS)
        caption_inv = jnp.concatenate([caption_inv] * images, axis=0)
        cosine = inner * mixed_inv * caption_inv
        logit = LOGIT_SCALE * cosine + LOGIT_BIAS
        label = jnp.where(owner_2 == image, 1.0, -1.0)
        slope = -LOGIT_SCALE * label / (1.0 + jnp.exp(label * logit))
        across = slope * mixed_inv * caption_inv
        grad_mixed = across * caption_2 - (slope * cosine * mixed_inv * mixed_inv) * mixed
        grad_pooled_t = dot_t(wo[...], grad_mixed.astype(BF16))
        if own:
            direct = across * mixed - (slope * cosine * caption_inv * caption_inv) * caption_2
            direct = sum(direct[i * block : (i + 1) * block] for i in range(images))

        grad_pooled = []
        means = []
        for i in range(images):
            scale = jnp.concatenate(
                [
                    jnp.broadcast_to(row, (HEAD_DIM, block))
                    for rows_ in inverse[i]
                    for row in by_head(rows_, block)
                ],
                axis=0,
            )
            found = (grad_pooled_t[:, i * block : (i + 1) * block] * scale).astype(BF16)
            grad_pooled.append(found.T)
            products = found.astype(F32) * jnp.concatenate(pooled_t[i], axis=0)
            products = [
                jnp.sum(products[h * HEAD_DIM : (h + 1) * HEAD_DIM], axis=0, keepdims=True)
                for h in range(d // HEAD_DIM)
            ]
            means.append(
                [
                    jnp.concatenate(
                        products[g * HEADS_IN_GROUP : (g + 1) * HEADS_IN_GROUP], axis=1
                    )
                    for g in range(groups)
                ]
            )

        def grad_weight(i, g):
            at, cols, _ = places(i, g)
            grads = head_stack(grad_pooled[i][:, cols])
            return grads, dot_t(values[at, cols], grads)

        grad_query = [None] * groups
        stacked_scores = [[] for _ in range(groups)]
        ahead = grad_weight(*units[0])
        for n, (i, g) in enumerate(units):
            at, cols, to = places(i, g)
            grads, grad_weights = ahead
            if n + 1 < len(units):
                ahead = grad_weight(*units[n + 1])
            weights = weights_ref[which, at, to].astype(F32)
            grad_scores = (weights * (grad_weights - means[i][g])).astype(BF16)
            stacked_scores[g].append(grad_scores)
            works = [
                functools.partial(
                    finish, gv, gv_b, at, cols, weights_ref.at[which, at, to], grads, which
                )
            ]
            if i + 1 == images:
                works.append(
                    functools.partial(
                        finish,
                        gk,
                        gk_b,
                        slice(0, images * patches),
                        cols,
                        jnp.concatenate(stacked_scores[g], axis=0),
                        queries[g],
                        which,
                    )
                )
            if own:
                later.extend(works)
                found = head_blocks(dot(keys_t[cols, at], grad_scores), block)
                grad_query[g] = found if grad_query[g] is None else grad_query[g] + found
            else:
                for work in works:
                    work()
        if own:
            grad_query = jnp.concatenate(grad_query, axis=0).T * HEAD_DIM**-0.5
            grad = direct + dot_t(grad_query.astype(BF16), wq[...])
            grad = grad.reshape(slots, rows, d)
            part[pl.ds(slot, slots)] = jnp.concatenate(
                [grad[:, :, :half], grad[:, :, half:]], axis=1
            ).astype(BF16)
        return later

    def finish(total, out, at, cols, left, right, which):
        add(total, out, at, cols, dot(left[...], right), which)

    def run_all(which, own, before=()):
        if blocks == 1:
            return run_block(0, which, own, before)

        @pl.loop(0, blocks)
        def _(n):
            for work in run_block(n * slots, which, own):
                work()

        return []

    later = run_all(0, True)

    @pl.loop(1, nb, unroll=unroll)
    def _(step):
        part_copy(step).start()

    for step in range(1, ns):
        span_copy(step, step).wait_recv()
        span_owner_copy(step, step).wait_recv()
        later = run_all(step, False, later)
    for work in later:
        work()
    if blocks > 1:
        gk_b[...] = gk[...].astype(BF16)
        gv_b[...] = gv[...].astype(BF16)
    token_out[...] = patches * (dot_t(gk_b[...], wk[...]) + dot_t(gv_b[...], wv[...]))

    all_parts.wait_recv()

    parts_in[me] = part[me]
    sum_out[...] = jnp.sum(parts_in[...].astype(F32), axis=0)

    all_caps.wait_send()
    all_owners.wait_send()
    all_parts.wait_send()

    for step in range(1, ns):
        span_copy(step, ns - step).wait_send()
        span_owner_copy(step, ns - step).wait_send()


def write_kernel(sum_ref, token_ref, caption_out, token_out, unfolded, sems):
    rows, d = caption_out.shape
    count = sems.shape[0] - 1
    chunk = token_ref.shape[0] // count
    copies = [
        pltpu.make_async_copy(
            token_ref.at[pl.ds(n * chunk, chunk)],
            token_out.at[pl.ds(n * chunk, chunk)],
            sems.at[n],
        )
        for n in range(count)
    ]
    for copy in copies:
        copy.start()
    summed = sum_ref[...] * CAPTION_SCALE
    unfolded[...] = jnp.concatenate([summed[:rows], summed[rows:]], axis=1)
    copies.append(pltpu.make_async_copy(unfolded, caption_out, sems.at[count]))
    copies[-1].start()
    for copy in copies:
        copy.wait()


def hold(x):
    return pltpu.with_memory_space_constraint(x, pltpu.HBM)


def on_device(nb, ns, image_tokens, captions, owner, w_query, w_key, w_value, w_out):
    images, patches, d = image_tokens.shape
    rows = captions.shape[0]
    total = images * patches
    block = math.gcd(nb * rows, LANES)
    vmem = pl.BlockSpec(memory_space=pltpu.VMEM)
    hbm = pl.BlockSpec(memory_space=pltpu.HBM)
    heads = d // HEAD_DIM
    dma = pltpu.SemaphoreType.DMA
    token_terms, summed = pl.pallas_call(
        functools.partial(pair_kernel, nb, ns, images),
        out_shape=(
            jax.ShapeDtypeStruct((total, d), F32),
            jax.ShapeDtypeStruct((2 * rows, d // 2), F32),
        ),
        in_specs=[hbm] * 7,
        out_specs=(vmem, vmem),
        scratch_shapes=[
            pltpu.VMEM((rows, d), BF16),
            pltpu.VMEM((1, rows), jnp.int32),
            pltpu.VMEM((total, d), BF16),
            pltpu.VMEM((d, d), BF16),
            pltpu.VMEM((d, d), BF16),
            pltpu.VMEM((d, d), BF16),
            pltpu.VMEM((d, d), BF16),
            pltpu.VMEM((total, d), BF16),
            pltpu.VMEM((total, d), BF16),
            pltpu.VMEM((d, total), BF16),
            pltpu.VMEM((d, total), BF16),
            pltpu.VMEM((ns, total, heads * block), BF16),
            pltpu.VMEM((total, d), F32),
            pltpu.VMEM((total, d), F32),
            pltpu.VMEM((total, d), BF16),
            pltpu.VMEM((total, d), BF16),
            pltpu.VMEM((ns, nb, 2 * rows, d // 2), BF16),
            pltpu.VMEM((ns, nb, 1, LANES), jnp.int32),
            pltpu.VMEM((nb, 2 * rows, d // 2), BF16),
            pltpu.VMEM((nb, 2 * rows, d // 2), BF16),
            dma((7,)),
            dma,
            dma,
            dma,
            dma,
            dma((ns,)),
            dma((ns,)),
            dma((ns,)),
            dma((ns,)),
            dma,
            dma,
        ],
        compiler_params=pltpu.CompilerParams(
            collective_id=0, has_side_effects=True, vmem_limit_bytes=36 * 2**20
        ),
        name="pairs",
    )(
        hold(captions),
        hold(owner.reshape(1, rows)),
        hold(image_tokens.reshape(total, d)),
        hold(w_query),
        hold(w_key),
        hold(w_value),
        hold(w_out),
    )
    caption_grad, token_grad = pl.pallas_call(
        write_kernel,
        out_shape=(
            jax.ShapeDtypeStruct((rows, d), F32),
            jax.ShapeDtypeStruct((total, d), F32),
        ),
        in_specs=[vmem, vmem],
        out_specs=(hbm, hbm),
        scratch_shapes=[
            pltpu.VMEM((rows, d), F32),
            dma((2 * images + 1,)),
        ],
        compiler_params=pltpu.CompilerParams(vmem_limit_bytes=16 * 2**20),
        name="write",
    )(summed, token_terms)
    return (caption_grad, token_grad.reshape(images, patches, d))


def solution(mesh):
    placed = (
        P("batch", None, None),
        P(("batch", "span"), None),
        P(("batch", "span")),
        P(),
        P(),
        P(),
        P(),
    )
    return jax.shard_map(
        functools.partial(on_device, mesh.shape["batch"], mesh.shape["span"]),
        mesh=mesh,
        in_specs=placed,
        out_specs=(P(("batch", "span"), None), P("batch", None, None)),
        check_vma=False,
    )
```

```python
import functools
import math

import jax
import jax.numpy as jnp
from jax import lax
from jax.experimental import pallas as pl
from jax.experimental.pallas import tpu as pltpu
from jax.sharding import PartitionSpec as P

HEAD_DIM = 64
LOGIT_SCALE = 10.0
LOGIT_BIAS = -2.0
NORM_EPS = 1e-06
CAPTION_SCALE = 16.0
LANES = 128
GROUP = 256
HEADS_IN_GROUP = GROUP // HEAD_DIM
F32 = jnp.float32
BF16 = jnp.bfloat16
MESH = pl.DeviceIdType.MESH


def dot(a, b):
    return jnp.dot(a, b, preferred_element_type=F32)


def dot_t(a, b):
    return lax.dot_general(a, b, (((1,), (1,)), ((), ())), preferred_element_type=F32)


def head_masks(tile):
    head = lax.broadcasted_iota(jnp.int32, (tile, GROUP), 1) // HEAD_DIM
    return [(head == h).astype(F32).astype(BF16) for h in range(HEADS_IN_GROUP)]


def head_stack(x):
    tile = math.gcd(x.shape[0], 16)
    tiles = x.reshape(x.shape[0] // tile, tile, GROUP)
    return jnp.concatenate([(tiles * m).reshape(x.shape) for m in head_masks(tile)], axis=0)


def head_blocks(x, width):
    return jnp.concatenate(
        [
            x[h * HEAD_DIM : (h + 1) * HEAD_DIM, h * width : (h + 1) * width]
            for h in range(HEADS_IN_GROUP)
        ],
        axis=0,
    )


def by_head(rows, width):
    return [rows[:, h * width : (h + 1) * width] for h in range(HEADS_IN_GROUP)]


def pair_kernel(
    nb,
    ns,
    images,
    captions_hbm,
    owner_hbm,
    tokens_hbm,
    wq_hbm,
    wk_hbm,
    wv_hbm,
    wo_hbm,
    token_out,
    sum_out,
    captions_ref,
    owner_ref,
    tokens,
    wq,
    wk,
    wv,
    wo,
    keys,
    values,
    keys_t,
    values_t,
    weights_ref,
    gk,
    gv,
    gk_b,
    gv_b,
    caps,
    owners,
    part,
    parts_in,
    load_sem,
    cap_send,
    cap_recv,
    owner_send,
    owner_recv,
    sibling_sems,
    span_send,
    span_recv,
    span_owner_send,
    span_owner_recv,
    part_send,
    part_recv,
):
    me = lax.axis_index("batch")
    my_span = lax.axis_index("span")
    rows = captions_ref.shape[0]
    d = captions_ref.shape[1]
    half = d // 2
    patches = tokens.shape[0] // images
    groups = d // GROUP
    block = math.gcd(nb * rows, LANES)
    slots = block // rows
    blocks = nb * rows // block
    stacked = HEADS_IN_GROUP * block
    unroll = nb <= 16

    cores = math.gcd(nb, 2)
    chips = nb // cores
    core = lax.rem(me, cores)
    chip = me // cores
    my_slot = core * chips + chip

    def peer_of(step):
        return lax.rem(me + step, nb)

    def slot_of(device):
        return lax.rem(device, cores) * chips + device // cores

    def twin_of(step):
        return lax.rem(chip + step, chips) * cores + core

    def sibling_of(step):
        return chip * cores + lax.rem(core + step, cores)

    def span_of(step):
        return lax.rem(my_span + step, ns)

    loads = [
        pltpu.make_async_copy(src, dst, load_sem.at[n])
        for n, (src, dst) in enumerate(
            (
                (captions_hbm, captions_ref),
                (owner_hbm, owner_ref),
                (tokens_hbm, tokens),
                (wk_hbm, wk),
                (wv_hbm, wv),
                (wq_hbm, wq),
                (wo_hbm, wo),
            )
        )
    ]
    for load in loads[:2]:
        load.start()

    barrier = pltpu.get_barrier_semaphore()

    @pl.loop(1, nb, unroll=unroll)
    def _(step):
        pl.semaphore_signal(
            barrier, inc=1, device_id={"batch": peer_of(step)}, device_id_type=MESH
        )

    for step in range(1, ns):
        pl.semaphore_signal(
            barrier, inc=1, device_id={"span": span_of(step)}, device_id_type=MESH
        )

    for load in loads[2:]:
        load.start()
    for load in loads[:2]:
        load.wait()
    mine = captions_ref[...].astype(F32)
    caps[0, my_slot] = jnp.concatenate([mine[:, :half], mine[:, half:]], axis=0).astype(BF16)
    owners[0, my_slot] = jnp.concatenate(
        [owner_ref[...], jnp.zeros((1, LANES - rows), jnp.int32)], axis=1
    )

    pl.semaphore_wait(barrier, nb + ns - 2)

    def cap_copy(step):
        return pltpu.make_async_remote_copy(
            src_ref=caps.at[0, my_slot],
            dst_ref=caps.at[0, my_slot],
            send_sem=cap_send,
            recv_sem=cap_recv,
            device_id={"batch": twin_of(step)},
            device_id_type=MESH,
        )

    def owner_copy(step):
        return pltpu.make_async_remote_copy(
            src_ref=owners.at[0, my_slot],
            dst_ref=owners.at[0, my_slot],
            send_sem=owner_send,
            recv_sem=owner_recv,
            device_id={"batch": twin_of(step)},
            device_id_type=MESH,
        )

    def part_copy(step):
        return pltpu.make_async_remote_copy(
            src_ref=part.at[slot_of(peer_of(step))],
            dst_ref=parts_in.at[my_slot],
            send_sem=part_send,
            recv_sem=part_recv,
            device_id={"batch": peer_of(step)},
            device_id_type=MESH,
        )

    def span_copy(step, slot):
        return pltpu.make_async_remote_copy(
            src_ref=caps.at[0],
            dst_ref=caps.at[ns - step],
            send_sem=span_send.at[step],
            recv_sem=span_recv.at[slot],
            device_id={"span": span_of(step)},
            device_id_type=MESH,
        )

    def whole(ref, count, send_sem, recv_sem):
        return pltpu.make_async_remote_copy(
            src_ref=ref.at[pl.ds(0, count)],
            dst_ref=ref.at[pl.ds(0, count)],
            send_sem=send_sem,
            recv_sem=recv_sem,
            device_id={"batch": peer_of(1)},
            device_id_type=MESH,
        )

    all_caps = whole(caps.at[0], chips - 1, cap_send, cap_recv)
    all_owners = whole(owners.at[0], chips - 1, owner_send, owner_recv)
    all_parts = whole(parts_in, nb - 1, part_send, part_recv)

    def sibling_copy(ref, step, sems, kind):
        ours = ref.at[0, pl.ds(core * chips, chips)]
        return pltpu.make_async_remote_copy(
            src_ref=ours,
            dst_ref=ours,
            send_sem=sems.at[0, kind, step],
            recv_sem=sems.at[1, kind, step],
            device_id={"batch": sibling_of(step)},
            device_id_type=MESH,
        )

    def span_owner_copy(step, slot):
        return pltpu.make_async_remote_copy(
            src_ref=owners.at[0],
            dst_ref=owners.at[ns - step],
            send_sem=span_owner_send.at[step],
            recv_sem=span_owner_recv.at[slot],
            device_id={"span": span_of(step)},
            device_id_type=MESH,
        )

    @pl.loop(1, chips, unroll=unroll)
    def _(step):
        cap_copy(step).start()

    @pl.loop(1, chips, unroll=unroll)
    def _(step):
        owner_copy(step).start()

    for load in loads[2:5]:
        load.wait()
    for i in range(images):
        at = pl.ds(i * patches, patches)
        found = dot(tokens[at, :], wk[...])
        keys[at, :] = found.astype(BF16)
        keys_t[:, at] = found.astype(BF16).T
        found = dot(tokens[at, :], wv[...])
        values[at, :] = found.astype(BF16)
        values_t[:, at] = found.astype(BF16).T
    if blocks > 1:
        gk[...] = jnp.zeros_like(gk)
        gv[...] = jnp.zeros_like(gv)
    for load in loads[5:]:
        load.wait()

    siblings = [
        [sibling_copy(ref, step, sibling_sems, kind) for step in range(1, cores)]
        for kind, ref in enumerate((caps, owners))
    ]
    all_caps.wait_recv()
    for copy in siblings[0]:
        copy.start()
    all_owners.wait_recv()
    for copy in siblings[1]:
        copy.start()
    for copy in siblings[0] + siblings[1]:
        copy.wait_recv()

    for step in range(1, ns):
        span_copy(step, ns - step).start()

    for step in range(1, ns):
        span_owner_copy(step, ns - step).start()

    def add(total, out, at, cols, found, which):
        if blocks > 1 or which > 0:
            found = total[at, cols] + found
        if blocks == 1 and which == ns - 1:
            out[at, cols] = found.astype(BF16)
        else:
            total[at, cols] = found

    def run_block(slot, which, own, before=()):
        later = []
        held = caps[which, pl.ds(slot, slots)].astype(F32)
        caption = jnp.concatenate(
            [
                held[:, :rows].reshape(block, half),
                held[:, rows:].reshape(block, half),
            ],
            axis=1,
        )
        owner = owners[which, pl.ds(slot, slots)]
        owner = jnp.broadcast_to(owner, (slots, rows, LANES))
        row = lax.broadcasted_iota(jnp.int32, owner.shape, 1)
        lane = lax.broadcasted_iota(jnp.int32, owner.shape, 2)
        owner = jnp.sum(
            jnp.where(row == lane, owner, 0).astype(F32).reshape(block, LANES),
            axis=1,
            keepdims=True,
        )
        query = (dot(caption.astype(BF16), wq[...]) * HEAD_DIM**-0.5).astype(BF16)
        queries = [head_stack(query[:, g * GROUP : (g + 1) * GROUP]) for g in range(groups)]

        units = [(i, g) for i in range(images) for g in range(groups)]

        def places(i, g):
            return (
                slice(i * patches, (i + 1) * patches),
                slice(g * GROUP, (g + 1) * GROUP),
                slice(g * stacked, (g + 1) * stacked),
            )

        def score(i, g):
            at, cols, _ = places(i, g)
            return dot_t(keys[at, cols], queries[g])

        pooled = [[] for _ in range(images)]
        inverse = [[] for _ in range(images)]
        ahead = score(*units[0])
        for n, (i, g) in enumerate(units):
            at, cols, to = places(i, g)
            scores = ahead
            if n + 1 < len(units):
                ahead = score(*units[n + 1])
            if n < len(before):
                before[n]()
            scores = jnp.exp(scores - jnp.max(scores, axis=0, keepdims=True))
            inverse[i].append(1.0 / jnp.sum(scores, axis=0, keepdims=True))
            weights = scores.astype(BF16)
            weights_ref[which, at, to] = weights
            pooled[i].append(head_blocks(dot(values_t[cols, at], weights) * inverse[i][g], block))
        pooled_t = pooled
        pooled = [jnp.concatenate(found, axis=0).T.astype(BF16) for found in pooled]
        mixed = dot(jnp.concatenate(pooled, axis=0), wo[...])
        caption_2 = jnp.concatenate([caption] * images, axis=0)
        owner_2 = jnp.concatenate([owner] * images, axis=0)
        image = (
            lax.broadcasted_iota(jnp.int32, (images * block, 1), 0) // block + me * images
        ).astype(F32)
        inner = jnp.sum(mixed * caption_2, axis=1, keepdims=True)
        mixed_inv = lax.rsqrt(jnp.sum(mixed * mixed, axis=1, keepdims=True) + NORM_EPS)
        caption_inv = lax.rsqrt(jnp.sum(caption * caption, axis=1, keepdims=True) + NORM_EPS)
        caption_inv = jnp.concatenate([caption_inv] * images, axis=0)
        cosine = inner * mixed_inv * caption_inv
        logit = LOGIT_SCALE * cosine + LOGIT_BIAS
        label = jnp.where(owner_2 == image, 1.0, -1.0)
        slope = -LOGIT_SCALE * label / (1.0 + jnp.exp(label * logit))
        across = slope * mixed_inv * caption_inv
        grad_mixed = across * caption_2 - (slope * cosine * mixed_inv * mixed_inv) * mixed
        grad_pooled_t = dot_t(wo[...], grad_mixed.astype(BF16))
        if own:
            direct = across * mixed - (slope * cosine * caption_inv * caption_inv) * caption_2
            direct = sum(direct[i * block : (i + 1) * block] for i in range(images))

        grad_pooled = []
        means = []
        for i in range(images):
            scale = jnp.concatenate(
                [
                    jnp.broadcast_to(row, (HEAD_DIM, block))
                    for rows_ in inverse[i]
                    for row in by_head(rows_, block)
                ],
                axis=0,
            )
            found = (grad_pooled_t[:, i * block : (i + 1) * block] * scale).astype(BF16)
            grad_pooled.append(found.T)
            products = found.astype(F32) * jnp.concatenate(pooled_t[i], axis=0)
            products = [
                jnp.sum(products[h * HEAD_DIM : (h + 1) * HEAD_DIM], axis=0, keepdims=True)
                for h in range(d // HEAD_DIM)
            ]
            means.append(
                [
                    jnp.concatenate(
                        products[g * HEADS_IN_GROUP : (g + 1) * HEADS_IN_GROUP], axis=1
                    )
                    for g in range(groups)
                ]
            )

        def grad_weight(i, g):
            at, cols, _ = places(i, g)
            grads = head_stack(grad_pooled[i][:, cols])
            return grads, dot_t(values[at, cols], grads)

        grad_query = [None] * groups
        ahead = grad_weight(*units[0])
        for n, (i, g) in enumerate(units):
            at, cols, to = places(i, g)
            grads, grad_weights = ahead
            if n + 1 < len(units):
                ahead = grad_weight(*units[n + 1])
            weights = weights_ref[which, at, to].astype(F32)
            grad_scores = (weights * (grad_weights - means[i][g])).astype(BF16)
            later.append(
                functools.partial(finish, at, cols, to, grads, grad_scores, queries[g], which)
            )
            if own:
                found = head_blocks(dot(keys_t[cols, at], grad_scores), block)
                grad_query[g] = found if grad_query[g] is None else grad_query[g] + found
            else:
                later.pop()()
                if blocks == 1 and which == ns - 1 and g == groups - 1:
                    token_product(at)
        if own:
            grad_query = jnp.concatenate(grad_query, axis=0).T * HEAD_DIM**-0.5
            grad = direct + dot_t(grad_query.astype(BF16), wq[...])
            grad = grad.reshape(slots, rows, d)
            part[pl.ds(slot, slots)] = jnp.concatenate(
                [grad[:, :, :half], grad[:, :, half:]], axis=1
            ).astype(BF16)
        return later

    def token_product(at):
        token_out[at, :] = patches * (dot_t(gk_b[at, :], wk[...]) + dot_t(gv_b[at, :], wv[...]))

    def finish(at, cols, to, grads, grad_scores, queries, which):
        add(gv, gv_b, at, cols, dot(weights_ref[which, at, to], grads), which)
        add(gk, gk_b, at, cols, dot(grad_scores, queries), which)

    def run_all(which, own, before=()):
        if blocks == 1:
            return run_block(0, which, own, before)

        @pl.loop(0, blocks)
        def _(n):
            for work in run_block(n * slots, which, own):
                work()

        return []

    later = run_all(0, True)

    @pl.loop(1, nb, unroll=unroll)
    def _(step):
        part_copy(step).start()

    for step in range(1, ns):
        span_copy(step, step).wait_recv()
        span_owner_copy(step, step).wait_recv()
        later = run_all(step, False, later)
    for work in later:
        work()
    if blocks > 1:
        gk_b[...] = gk[...].astype(BF16)
        gv_b[...] = gv[...].astype(BF16)
    if blocks > 1 or ns == 1:
        for i in range(images):
            token_product(slice(i * patches, (i + 1) * patches))

    all_parts.wait_recv()

    parts_in[my_slot] = part[my_slot]
    sum_out[...] = jnp.sum(parts_in[...].astype(F32), axis=0)

    all_caps.wait_send()
    for copy in siblings[0] + siblings[1]:
        copy.wait_send()
    all_owners.wait_send()
    all_parts.wait_send()

    for step in range(1, ns):
        span_copy(step, ns - step).wait_send()
        span_owner_copy(step, ns - step).wait_send()


def write_kernel(sum_ref, token_ref, caption_out, token_out, unfolded, sems):
    rows, d = caption_out.shape
    count = sems.shape[0] - 1
    chunk = token_ref.shape[0] // count
    copies = [
        pltpu.make_async_copy(
            token_ref.at[pl.ds(n * chunk, chunk)],
            token_out.at[pl.ds(n * chunk, chunk)],
            sems.at[n],
        )
        for n in range(count)
    ]
    for copy in copies:
        copy.start()
    summed = sum_ref[...] * CAPTION_SCALE
    unfolded[...] = jnp.concatenate([summed[:rows], summed[rows:]], axis=1)
    copies.append(pltpu.make_async_copy(unfolded, caption_out, sems.at[count]))
    copies[-1].start()
    for copy in copies:
        copy.wait()


def hold(x):
    return pltpu.with_memory_space_constraint(x, pltpu.HBM)


def on_device(nb, ns, image_tokens, captions, owner, w_query, w_key, w_value, w_out):
    images, patches, d = image_tokens.shape
    rows = captions.shape[0]
    total = images * patches
    block = math.gcd(nb * rows, LANES)
    vmem = pl.BlockSpec(memory_space=pltpu.VMEM)
    hbm = pl.BlockSpec(memory_space=pltpu.HBM)
    heads = d // HEAD_DIM
    dma = pltpu.SemaphoreType.DMA
    token_terms, summed = pl.pallas_call(
        functools.partial(pair_kernel, nb, ns, images),
        out_shape=(
            jax.ShapeDtypeStruct((total, d), F32),
            jax.ShapeDtypeStruct((2 * rows, d // 2), F32),
        ),
        in_specs=[hbm] * 7,
        out_specs=(vmem, vmem),
        scratch_shapes=[
            pltpu.VMEM((rows, d), BF16),
            pltpu.VMEM((1, rows), jnp.int32),
            pltpu.VMEM((total, d), BF16),
            pltpu.VMEM((d, d), BF16),
            pltpu.VMEM((d, d), BF16),
            pltpu.VMEM((d, d), BF16),
            pltpu.VMEM((d, d), BF16),
            pltpu.VMEM((total, d), BF16),
            pltpu.VMEM((total, d), BF16),
            pltpu.VMEM((d, total), BF16),
            pltpu.VMEM((d, total), BF16),
            pltpu.VMEM((ns, total, heads * block), BF16),
            pltpu.VMEM((total, d), F32),
            pltpu.VMEM((total, d), F32),
            pltpu.VMEM((total, d), BF16),
            pltpu.VMEM((total, d), BF16),
            pltpu.VMEM((ns, nb, 2 * rows, d // 2), BF16),
            pltpu.VMEM((ns, nb, 1, LANES), jnp.int32),
            pltpu.VMEM((nb, 2 * rows, d // 2), BF16),
            pltpu.VMEM((nb, 2 * rows, d // 2), BF16),
            dma((7,)),
            dma,
            dma,
            dma,
            dma,
            dma((2, 2, 2)),
            dma((ns,)),
            dma((ns,)),
            dma((ns,)),
            dma((ns,)),
            dma,
            dma,
        ],
        compiler_params=pltpu.CompilerParams(
            collective_id=0, has_side_effects=True, vmem_limit_bytes=36 * 2**20
        ),
        name="pairs",
    )(
        hold(captions),
        hold(owner.reshape(1, rows)),
        hold(image_tokens.reshape(total, d)),
        hold(w_query),
        hold(w_key),
        hold(w_value),
        hold(w_out),
    )
    caption_grad, token_grad = pl.pallas_call(
        write_kernel,
        out_shape=(
            jax.ShapeDtypeStruct((rows, d), F32),
            jax.ShapeDtypeStruct((total, d), F32),
        ),
        in_specs=[vmem, vmem],
        out_specs=(hbm, hbm),
        scratch_shapes=[
            pltpu.VMEM((rows, d), F32),
            dma((2 * images + 1,)),
        ],
        compiler_params=pltpu.CompilerParams(vmem_limit_bytes=16 * 2**20),
        name="write",
    )(summed, token_terms)
    return (caption_grad, token_grad.reshape(images, patches, d))


def solution(mesh):
    placed = (
        P("batch", None, None),
        P(("batch", "span"), None),
        P(("batch", "span")),
        P(),
        P(),
        P(),
        P(),
    )
    return jax.shard_map(
        functools.partial(on_device, mesh.shape["batch"], mesh.shape["span"]),
        mesh=mesh,
        in_specs=placed,
        out_specs=(P(("batch", "span"), None), P("batch", None, None)),
        check_vma=False,
    )
```

```python
import functools
import math

import jax
import jax.numpy as jnp
from jax import lax
from jax.experimental import pallas as pl
from jax.experimental.pallas import tpu as pltpu
from jax.sharding import PartitionSpec as P

HEAD_DIM = 64
LOGIT_SCALE = 10.0
LOGIT_BIAS = -2.0
NORM_EPS = 1e-06
CAPTION_SCALE = 16.0
LANES = 128
GROUP = 256
HEADS_IN_GROUP = GROUP // HEAD_DIM
F32 = jnp.float32
BF16 = jnp.bfloat16
MESH = pl.DeviceIdType.MESH


def dot(a, b):
    return jnp.dot(a, b, preferred_element_type=F32)


def dot_t(a, b):
    return lax.dot_general(a, b, (((1,), (1,)), ((), ())), preferred_element_type=F32)


def head_masks(tile):
    head = lax.broadcasted_iota(jnp.int32, (tile, GROUP), 1) // HEAD_DIM
    return [(head == h).astype(F32).astype(BF16) for h in range(HEADS_IN_GROUP)]


def head_stack(x):
    tile = math.gcd(x.shape[0], 16)
    tiles = x.reshape(x.shape[0] // tile, tile, GROUP)
    return jnp.concatenate([(tiles * m).reshape(x.shape) for m in head_masks(tile)], axis=0)


def head_blocks(x, width):
    return jnp.concatenate(
        [
            x[h * HEAD_DIM : (h + 1) * HEAD_DIM, h * width : (h + 1) * width]
            for h in range(HEADS_IN_GROUP)
        ],
        axis=0,
    )


def by_head(rows, width):
    return [rows[:, h * width : (h + 1) * width] for h in range(HEADS_IN_GROUP)]


def pair_kernel(
    nb,
    ns,
    images,
    captions_hbm,
    owner_hbm,
    tokens_hbm,
    wq_hbm,
    wk_hbm,
    wv_hbm,
    wo_hbm,
    token_out,
    sum_out,
    captions_ref,
    owner_ref,
    tokens,
    wq,
    wk,
    wv,
    wo,
    keys,
    values,
    keys_t,
    values_t,
    weights_ref,
    gk,
    gv,
    gk_b,
    gv_b,
    caps,
    owners,
    part,
    parts_in,
    load_sem,
    cap_send,
    cap_recv,
    owner_send,
    owner_recv,
    span_send,
    span_recv,
    span_owner_send,
    span_owner_recv,
    part_send,
    part_recv,
):
    me = lax.axis_index("batch")
    my_span = lax.axis_index("span")
    rows = captions_ref.shape[0]
    d = captions_ref.shape[1]
    half = d // 2
    patches = tokens.shape[0] // images
    groups = d // GROUP
    block = math.gcd(nb * rows, LANES)
    slots = block // rows
    blocks = nb * rows // block
    stacked = HEADS_IN_GROUP * block
    unroll = nb <= 16

    def peer_of(step):
        return lax.rem(me + step, nb)

    def span_of(step):
        return lax.rem(my_span + step, ns)

    loads = [
        pltpu.make_async_copy(src, dst, load_sem.at[n])
        for n, (src, dst) in enumerate(
            (
                (captions_hbm, captions_ref),
                (owner_hbm, owner_ref),
                (tokens_hbm, tokens),
                (wk_hbm, wk),
                (wv_hbm, wv),
                (wq_hbm, wq),
                (wo_hbm, wo),
            )
        )
    ]
    for load in loads[:2]:
        load.start()

    barrier = pltpu.get_barrier_semaphore()

    @pl.loop(1, nb, unroll=unroll)
    def _(step):
        pl.semaphore_signal(
            barrier, inc=1, device_id={"batch": peer_of(step)}, device_id_type=MESH
        )

    for step in range(1, ns):
        pl.semaphore_signal(
            barrier, inc=1, device_id={"span": span_of(step)}, device_id_type=MESH
        )

    for load in loads[2:]:
        load.start()
    for load in loads[:2]:
        load.wait()
    mine = captions_ref[...].astype(F32)
    caps[0, me] = jnp.concatenate([mine[:, :half], mine[:, half:]], axis=0).astype(BF16)
    owners[0, me] = jnp.concatenate(
        [owner_ref[...], jnp.zeros((1, LANES - rows), jnp.int32)], axis=1
    )

    pl.semaphore_wait(barrier, nb + ns - 2)

    def cap_copy(step):
        return pltpu.make_async_remote_copy(
            src_ref=caps.at[0, me],
            dst_ref=caps.at[0, me],
            send_sem=cap_send,
            recv_sem=cap_recv,
            device_id={"batch": peer_of(step)},
            device_id_type=MESH,
        )

    def owner_copy(step):
        return pltpu.make_async_remote_copy(
            src_ref=owners.at[0, me],
            dst_ref=owners.at[0, me],
            send_sem=owner_send,
            recv_sem=owner_recv,
            device_id={"batch": peer_of(step)},
            device_id_type=MESH,
        )

    def part_copy(step):
        return pltpu.make_async_remote_copy(
            src_ref=part.at[peer_of(step)],
            dst_ref=parts_in.at[me],
            send_sem=part_send,
            recv_sem=part_recv,
            device_id={"batch": peer_of(step)},
            device_id_type=MESH,
        )

    def span_copy(step, slot):
        return pltpu.make_async_remote_copy(
            src_ref=caps.at[0],
            dst_ref=caps.at[ns - step],
            send_sem=span_send.at[step],
            recv_sem=span_recv.at[slot],
            device_id={"span": span_of(step)},
            device_id_type=MESH,
        )

    def whole(ref, send_sem, recv_sem):
        return pltpu.make_async_remote_copy(
            src_ref=ref.at[pl.ds(0, nb - 1)],
            dst_ref=ref.at[pl.ds(0, nb - 1)],
            send_sem=send_sem,
            recv_sem=recv_sem,
            device_id={"batch": peer_of(1)},
            device_id_type=MESH,
        )

    all_caps = whole(caps.at[0], cap_send, cap_recv)
    all_owners = whole(owners.at[0], owner_send, owner_recv)
    all_parts = whole(parts_in, part_send, part_recv)

    def span_owner_copy(step, slot):
        return pltpu.make_async_remote_copy(
            src_ref=owners.at[0],
            dst_ref=owners.at[ns - step],
            send_sem=span_owner_send.at[step],
            recv_sem=span_owner_recv.at[slot],
            device_id={"span": span_of(step)},
            device_id_type=MESH,
        )

    @pl.loop(1, nb, unroll=unroll)
    def _(step):
        cap_copy(step).start()

    for load in loads[2:5]:
        load.wait()
    for i in range(images):
        at = pl.ds(i * patches, patches)
        found = dot(tokens[at, :], wk[...])
        keys[at, :] = found.astype(BF16)
        found = dot(tokens[at, :], wv[...])
        values[at, :] = found.astype(BF16)
        values_t[:, at] = found.astype(BF16).T

    @pl.loop(1, nb, unroll=unroll)
    def _(step):
        owner_copy(step).start()

    if blocks > 1:
        gk[...] = jnp.zeros_like(gk)
        gv[...] = jnp.zeros_like(gv)
    for load in loads[5:]:
        load.wait()

    all_caps.wait_recv()

    for step in range(1, ns):
        span_copy(step, ns - step).start()

    def turn_keys(i):
        at = slice(i * patches, (i + 1) * patches)
        keys_t[:, at] = keys[at, :].T

    def pass_owners():
        all_owners.wait_recv()
        for step in range(1, ns):
            span_owner_copy(step, ns - step).start()

    def add(total, out, at, cols, found, which):
        if blocks > 1 or which > 0:
            found = total[at, cols] + found
        if blocks == 1 and which == ns - 1:
            out[at, cols] = found.astype(BF16)
        else:
            total[at, cols] = found

    def run_block(slot, which, own, before=(), arrive=None):
        later = []
        held = caps[which, pl.ds(slot, slots)].astype(F32)
        caption = jnp.concatenate(
            [
                held[:, :rows].reshape(block, half),
                held[:, rows:].reshape(block, half),
            ],
            axis=1,
        )
        query = (dot(caption.astype(BF16), wq[...]) * HEAD_DIM**-0.5).astype(BF16)
        queries = [head_stack(query[:, g * GROUP : (g + 1) * GROUP]) for g in range(groups)]

        units = [(i, g) for i in range(images) for g in range(groups)]

        def places(i, g):
            return (
                slice(i * patches, (i + 1) * patches),
                slice(g * GROUP, (g + 1) * GROUP),
                slice(g * stacked, (g + 1) * stacked),
            )

        def score(i, g):
            at, cols, _ = places(i, g)
            return dot_t(keys[at, cols], queries[g])

        pooled = [[] for _ in range(images)]
        inverse = [[] for _ in range(images)]
        ahead = score(*units[0])
        for n, (i, g) in enumerate(units):
            at, cols, to = places(i, g)
            scores = ahead
            if n + 1 < len(units):
                ahead = score(*units[n + 1])
            if n < len(before):
                before[n]()
            scores = jnp.exp(scores - jnp.max(scores, axis=0, keepdims=True))
            inverse[i].append(1.0 / jnp.sum(scores, axis=0, keepdims=True))
            weights = scores.astype(BF16)
            weights_ref[which, at, to] = weights
            pooled[i].append(head_blocks(dot(values_t[cols, at], weights) * inverse[i][g], block))
        pooled_t = pooled
        pooled = [jnp.concatenate(found, axis=0).T.astype(BF16) for found in pooled]
        if arrive is not None:
            arrive()
        owner = owners[which, pl.ds(slot, slots)]
        owner = jnp.broadcast_to(owner, (slots, rows, LANES))
        row = lax.broadcasted_iota(jnp.int32, owner.shape, 1)
        lane = lax.broadcasted_iota(jnp.int32, owner.shape, 2)
        owner = jnp.sum(
            jnp.where(row == lane, owner, 0).astype(F32).reshape(block, LANES),
            axis=1,
            keepdims=True,
        )
        mixed = dot(jnp.concatenate(pooled, axis=0), wo[...])
        caption_2 = jnp.concatenate([caption] * images, axis=0)
        owner_2 = jnp.concatenate([owner] * images, axis=0)
        image = (
            lax.broadcasted_iota(jnp.int32, (images * block, 1), 0) // block + me * images
        ).astype(F32)
        inner = jnp.sum(mixed * caption_2, axis=1, keepdims=True)
        mixed_inv = lax.rsqrt(jnp.sum(mixed * mixed, axis=1, keepdims=True) + NORM_EPS)
        caption_inv = lax.rsqrt(jnp.sum(caption * caption, axis=1, keepdims=True) + NORM_EPS)
        caption_inv = jnp.concatenate([caption_inv] * images, axis=0)
        cosine = inner * mixed_inv * caption_inv
        logit = LOGIT_SCALE * cosine + LOGIT_BIAS
        label = jnp.where(owner_2 == image, 1.0, -1.0)
        slope = -LOGIT_SCALE * label / (1.0 + jnp.exp(label * logit))
        across = slope * mixed_inv * caption_inv
        grad_mixed = across * caption_2 - (slope * cosine * mixed_inv * mixed_inv) * mixed
        grad_pooled_t = dot_t(wo[...], grad_mixed.astype(BF16))
        if own:
            direct = across * mixed - (slope * cosine * caption_inv * caption_inv) * caption_2
            direct = sum(direct[i * block : (i + 1) * block] for i in range(images))

        grad_pooled = []
        means = []
        for i in range(images):
            scale = jnp.concatenate(
                [
                    jnp.broadcast_to(row, (HEAD_DIM, block))
                    for rows_ in inverse[i]
                    for row in by_head(rows_, block)
                ],
                axis=0,
            )
            found = (grad_pooled_t[:, i * block : (i + 1) * block] * scale).astype(BF16)
            grad_pooled.append(found.T)
            products = found.astype(F32) * jnp.concatenate(pooled_t[i], axis=0)
            products = [
                jnp.sum(products[h * HEAD_DIM : (h + 1) * HEAD_DIM], axis=0, keepdims=True)
                for h in range(d // HEAD_DIM)
            ]
            means.append(
                [
                    jnp.concatenate(
                        products[g * HEADS_IN_GROUP : (g + 1) * HEADS_IN_GROUP], axis=1
                    )
                    for g in range(groups)
                ]
            )

        def grad_weight(i, g):
            at, cols, _ = places(i, g)
            grads = head_stack(grad_pooled[i][:, cols])
            return grads, dot_t(values[at, cols], grads)

        grad_query = [None] * groups
        ahead = grad_weight(*units[0])
        for n, (i, g) in enumerate(units):
            at, cols, to = places(i, g)
            grads, grad_weights = ahead
            if n + 1 < len(units):
                ahead = grad_weight(*units[n + 1])
            weights = weights_ref[which, at, to].astype(F32)
            grad_scores = (weights * (grad_weights - means[i][g])).astype(BF16)
            later.append(
                functools.partial(finish, at, cols, to, grads, grad_scores, queries[g], which)
            )
            if own:
                found = head_blocks(dot(keys_t[cols, at], grad_scores), block)
                grad_query[g] = found if grad_query[g] is None else grad_query[g] + found
            else:
                later.pop()()
                if blocks == 1 and which == ns - 1 and g == groups - 1:
                    token_product(at)
        if own:
            grad_query = jnp.concatenate(grad_query, axis=0).T * HEAD_DIM**-0.5
            grad = direct + dot_t(grad_query.astype(BF16), wq[...])
            grad = grad.reshape(slots, rows, d)
            part[pl.ds(slot, slots)] = jnp.concatenate(
                [grad[:, :, :half], grad[:, :, half:]], axis=1
            ).astype(BF16)
        return later

    def token_product(at):
        token_out[at, :] = patches * (dot_t(gk_b[at, :], wk[...]) + dot_t(gv_b[at, :], wv[...]))

    def finish(at, cols, to, grads, grad_scores, queries, which):
        add(gv, gv_b, at, cols, dot(weights_ref[which, at, to], grads), which)
        add(gk, gk_b, at, cols, dot(grad_scores, queries), which)

    def run_all(which, own, before=(), arrive=None):
        if blocks == 1:
            return run_block(0, which, own, before, arrive)

        for work in before:
            work()
        if arrive is not None:
            arrive()

        @pl.loop(0, blocks)
        def _(n):
            for work in run_block(n * slots, which, own):
                work()

        return []

    turns = [functools.partial(turn_keys, i) for i in range(images)]
    later = run_all(0, True, turns, pass_owners)

    @pl.loop(1, nb, unroll=unroll)
    def _(step):
        part_copy(step).start()

    for step in range(1, ns):
        span_copy(step, step).wait_recv()
        span_owner_copy(step, step).wait_recv()
        later = run_all(step, False, later)
    for work in later:
        work()
    if blocks > 1:
        gk_b[...] = gk[...].astype(BF16)
        gv_b[...] = gv[...].astype(BF16)
    if blocks > 1 or ns == 1:
        for i in range(images):
            token_product(slice(i * patches, (i + 1) * patches))

    all_parts.wait_recv()

    parts_in[me] = part[me]
    sum_out[...] = jnp.sum(parts_in[...].astype(F32), axis=0)

    all_caps.wait_send()
    all_owners.wait_send()
    all_parts.wait_send()

    for step in range(1, ns):
        span_copy(step, ns - step).wait_send()
        span_owner_copy(step, ns - step).wait_send()


def write_kernel(sum_ref, token_ref, caption_out, token_out, unfolded, sems):
    rows, d = caption_out.shape
    count = sems.shape[0] - 1
    chunk = token_ref.shape[0] // count
    copies = [
        pltpu.make_async_copy(
            token_ref.at[pl.ds(n * chunk, chunk)],
            token_out.at[pl.ds(n * chunk, chunk)],
            sems.at[n],
        )
        for n in range(count)
    ]
    for copy in copies:
        copy.start()
    summed = sum_ref[...] * CAPTION_SCALE
    unfolded[...] = jnp.concatenate([summed[:rows], summed[rows:]], axis=1)
    copies.append(pltpu.make_async_copy(unfolded, caption_out, sems.at[count]))
    copies[-1].start()
    for copy in copies:
        copy.wait()


def hold(x):
    return pltpu.with_memory_space_constraint(x, pltpu.HBM)


def on_device(nb, ns, image_tokens, captions, owner, w_query, w_key, w_value, w_out):
    images, patches, d = image_tokens.shape
    rows = captions.shape[0]
    total = images * patches
    block = math.gcd(nb * rows, LANES)
    vmem = pl.BlockSpec(memory_space=pltpu.VMEM)
    hbm = pl.BlockSpec(memory_space=pltpu.HBM)
    heads = d // HEAD_DIM
    dma = pltpu.SemaphoreType.DMA
    token_terms, summed = pl.pallas_call(
        functools.partial(pair_kernel, nb, ns, images),
        out_shape=(
            jax.ShapeDtypeStruct((total, d), F32),
            jax.ShapeDtypeStruct((2 * rows, d // 2), F32),
        ),
        in_specs=[hbm] * 7,
        out_specs=(vmem, vmem),
        scratch_shapes=[
            pltpu.VMEM((rows, d), BF16),
            pltpu.VMEM((1, rows), jnp.int32),
            pltpu.VMEM((total, d), BF16),
            pltpu.VMEM((d, d), BF16),
            pltpu.VMEM((d, d), BF16),
            pltpu.VMEM((d, d), BF16),
            pltpu.VMEM((d, d), BF16),
            pltpu.VMEM((total, d), BF16),
            pltpu.VMEM((total, d), BF16),
            pltpu.VMEM((d, total), BF16),
            pltpu.VMEM((d, total), BF16),
            pltpu.VMEM((ns, total, heads * block), BF16),
            pltpu.VMEM((total, d), F32),
            pltpu.VMEM((total, d), F32),
            pltpu.VMEM((total, d), BF16),
            pltpu.VMEM((total, d), BF16),
            pltpu.VMEM((ns, nb, 2 * rows, d // 2), BF16),
            pltpu.VMEM((ns, nb, 1, LANES), jnp.int32),
            pltpu.VMEM((nb, 2 * rows, d // 2), BF16),
            pltpu.VMEM((nb, 2 * rows, d // 2), BF16),
            dma((7,)),
            dma,
            dma,
            dma,
            dma,
            dma((ns,)),
            dma((ns,)),
            dma((ns,)),
            dma((ns,)),
            dma,
            dma,
        ],
        compiler_params=pltpu.CompilerParams(
            collective_id=0, has_side_effects=True, vmem_limit_bytes=36 * 2**20
        ),
        name="pairs",
    )(
        hold(captions),
        hold(owner.reshape(1, rows)),
        hold(image_tokens.reshape(total, d)),
        hold(w_query),
        hold(w_key),
        hold(w_value),
        hold(w_out),
    )
    caption_grad, token_grad = pl.pallas_call(
        write_kernel,
        out_shape=(
            jax.ShapeDtypeStruct((rows, d), F32),
            jax.ShapeDtypeStruct((total, d), F32),
        ),
        in_specs=[vmem, vmem],
        out_specs=(hbm, hbm),
        scratch_shapes=[
            pltpu.VMEM((rows, d), F32),
            dma((2 * images + 1,)),
        ],
        compiler_params=pltpu.CompilerParams(vmem_limit_bytes=16 * 2**20),
        name="write",
    )(summed, token_terms)
    return (caption_grad, token_grad.reshape(images, patches, d))


def solution(mesh):
    placed = (
        P("batch", None, None),
        P(("batch", "span"), None),
        P(("batch", "span")),
        P(),
        P(),
        P(),
        P(),
    )
    return jax.shard_map(
        functools.partial(on_device, mesh.shape["batch"], mesh.shape["span"]),
        mesh=mesh,
        in_specs=placed,
        out_specs=(P(("batch", "span"), None), P("batch", None, None)),
        check_vma=False,
    )
```

```python
import functools
import math

import jax
import jax.numpy as jnp
from jax import lax
from jax.experimental import pallas as pl
from jax.experimental.pallas import tpu as pltpu
from jax.sharding import PartitionSpec as P

HEAD_DIM = 64
LOGIT_SCALE = 10.0
LOGIT_BIAS = -2.0
NORM_EPS = 1e-06
CAPTION_SCALE = 16.0
LANES = 128
GROUP = 256
HEADS_IN_GROUP = GROUP // HEAD_DIM
F32 = jnp.float32
BF16 = jnp.bfloat16
MESH = pl.DeviceIdType.MESH


def dot(a, b):
    return jnp.dot(a, b, preferred_element_type=F32)


def dot_t(a, b):
    return lax.dot_general(a, b, (((1,), (1,)), ((), ())), preferred_element_type=F32)


def head_masks(tile):
    head = lax.broadcasted_iota(jnp.int32, (tile, GROUP), 1) // HEAD_DIM
    return [(head == h).astype(F32).astype(BF16) for h in range(HEADS_IN_GROUP)]


def head_stack(x):
    tile = math.gcd(x.shape[0], 16)
    tiles = x.reshape(x.shape[0] // tile, tile, GROUP)
    return jnp.concatenate([(tiles * m).reshape(x.shape) for m in head_masks(tile)], axis=0)


def head_blocks(x, width):
    return jnp.concatenate(
        [
            x[h * HEAD_DIM : (h + 1) * HEAD_DIM, h * width : (h + 1) * width]
            for h in range(HEADS_IN_GROUP)
        ],
        axis=0,
    )


def by_head(rows, width):
    return [rows[:, h * width : (h + 1) * width] for h in range(HEADS_IN_GROUP)]


def pair_kernel(
    nb,
    ns,
    images,
    captions_hbm,
    owner_hbm,
    tokens_hbm,
    wq_hbm,
    wk_hbm,
    wv_hbm,
    wo_hbm,
    token_out,
    sum_out,
    captions_ref,
    owner_ref,
    tokens,
    wq,
    wk,
    wv,
    wo,
    keys,
    values,
    keys_t,
    values_t,
    weights_ref,
    gk,
    gv,
    gk_b,
    gv_b,
    caps,
    owners,
    part,
    parts_in,
    load_sem,
    cap_send,
    cap_recv,
    owner_send,
    owner_recv,
    span_send,
    span_recv,
    span_owner_send,
    span_owner_recv,
    part_send,
    part_recv,
):
    me = lax.axis_index("batch")
    my_span = lax.axis_index("span")
    rows = captions_ref.shape[0]
    d = captions_ref.shape[1]
    half = d // 2
    patches = tokens.shape[0] // images
    groups = d // GROUP
    block = math.gcd(nb * rows, LANES)
    slots = block // rows
    blocks = nb * rows // block
    stacked = HEADS_IN_GROUP * block
    unroll = nb <= 16

    def peer_of(step):
        return lax.rem(me + step, nb)

    def span_of(step):
        return lax.rem(my_span + step, ns)

    loads = [
        pltpu.make_async_copy(src, dst, load_sem.at[n])
        for n, (src, dst) in enumerate(
            (
                (captions_hbm, captions_ref),
                (owner_hbm, owner_ref),
                (tokens_hbm, tokens),
                (wk_hbm, wk),
                (wv_hbm, wv),
                (wq_hbm, wq),
                (wo_hbm, wo),
            )
        )
    ]
    for load in loads[:2]:
        load.start()

    barrier = pltpu.get_barrier_semaphore()

    @pl.loop(1, nb, unroll=unroll)
    def _(step):
        pl.semaphore_signal(
            barrier, inc=1, device_id={"batch": peer_of(step)}, device_id_type=MESH
        )

    for step in range(1, ns):
        pl.semaphore_signal(
            barrier, inc=1, device_id={"span": span_of(step)}, device_id_type=MESH
        )

    for load in loads[2:]:
        load.start()
    for load in loads[:2]:
        load.wait()
    mine = captions_ref[...].astype(F32)
    caps[0, me] = jnp.concatenate([mine[:, :half], mine[:, half:]], axis=0).astype(BF16)
    owners[0, me] = jnp.concatenate(
        [owner_ref[...], jnp.zeros((1, LANES - rows), jnp.int32)], axis=1
    )

    pl.semaphore_wait(barrier, nb + ns - 2)

    def cap_copy(step):
        return pltpu.make_async_remote_copy(
            src_ref=caps.at[0, me],
            dst_ref=caps.at[0, me],
            send_sem=cap_send,
            recv_sem=cap_recv,
            device_id={"batch": peer_of(step)},
            device_id_type=MESH,
        )

    def owner_copy(step):
        return pltpu.make_async_remote_copy(
            src_ref=owners.at[0, me],
            dst_ref=owners.at[0, me],
            send_sem=owner_send,
            recv_sem=owner_recv,
            device_id={"batch": peer_of(step)},
            device_id_type=MESH,
        )

    def part_copy(step):
        return pltpu.make_async_remote_copy(
            src_ref=part.at[peer_of(step)],
            dst_ref=parts_in.at[me],
            send_sem=part_send,
            recv_sem=part_recv,
            device_id={"batch": peer_of(step)},
            device_id_type=MESH,
        )

    def span_copy(step, slot):
        return pltpu.make_async_remote_copy(
            src_ref=caps.at[0],
            dst_ref=caps.at[ns - step],
            send_sem=span_send.at[step],
            recv_sem=span_recv.at[slot],
            device_id={"span": span_of(step)},
            device_id_type=MESH,
        )

    def whole(ref, send_sem, recv_sem):
        return pltpu.make_async_remote_copy(
            src_ref=ref.at[pl.ds(0, nb - 1)],
            dst_ref=ref.at[pl.ds(0, nb - 1)],
            send_sem=send_sem,
            recv_sem=recv_sem,
            device_id={"batch": peer_of(1)},
            device_id_type=MESH,
        )

    all_caps = whole(caps.at[0], cap_send, cap_recv)
    all_owners = whole(owners.at[0], owner_send, owner_recv)
    all_parts = whole(parts_in, part_send, part_recv)

    def span_owner_copy(step, slot):
        return pltpu.make_async_remote_copy(
            src_ref=owners.at[0],
            dst_ref=owners.at[ns - step],
            send_sem=span_owner_send.at[step],
            recv_sem=span_owner_recv.at[slot],
            device_id={"span": span_of(step)},
            device_id_type=MESH,
        )

    @pl.loop(1, nb, unroll=unroll)
    def _(step):
        cap_copy(step).start()

    @pl.loop(1, nb, unroll=unroll)
    def _(step):
        owner_copy(step).start()

    for load in loads[2:5]:
        load.wait()
    for i in range(images):
        at = pl.ds(i * patches, patches)
        found = dot(tokens[at, :], wk[...])
        keys[at, :] = found.astype(BF16)
        keys_t[:, at] = found.astype(BF16).T
        found = dot(tokens[at, :], wv[...])
        values[at, :] = found.astype(BF16)
        values_t[:, at] = found.astype(BF16).T
    if blocks > 1:
        gk[...] = jnp.zeros_like(gk)
        gv[...] = jnp.zeros_like(gv)
    for load in loads[5:]:
        load.wait()

    all_caps.wait_recv()

    for step in range(1, ns):
        span_copy(step, ns - step).start()

    all_owners.wait_recv()

    for step in range(1, ns):
        span_owner_copy(step, ns - step).start()

    def add(total, out, at, cols, found, which):
        if blocks > 1 or which > 0:
            found = total[at, cols] + found
        if blocks == 1 and which == ns - 1:
            out[at, cols] = found.astype(BF16)
        else:
            total[at, cols] = found

    def run_block(slot, which, own, before=()):
        later = []
        held = caps[which, pl.ds(slot, slots)].astype(F32)
        caption = jnp.concatenate(
            [
                held[:, :rows].reshape(block, half),
                held[:, rows:].reshape(block, half),
            ],
            axis=1,
        )
        owner = owners[which, pl.ds(slot, slots)]
        owner = jnp.broadcast_to(owner, (slots, rows, LANES))
        row = lax.broadcasted_iota(jnp.int32, owner.shape, 1)
        lane = lax.broadcasted_iota(jnp.int32, owner.shape, 2)
        owner = jnp.sum(
            jnp.where(row == lane, owner, 0).astype(F32).reshape(block, LANES),
            axis=1,
            keepdims=True,
        )
        query = (dot(caption.astype(BF16), wq[...]) * HEAD_DIM**-0.5).astype(BF16)
        queries = [head_stack(query[:, g * GROUP : (g + 1) * GROUP]) for g in range(groups)]

        units = [(i, g) for i in range(images) for g in range(groups)]

        def places(i, g):
            return (
                slice(i * patches, (i + 1) * patches),
                slice(g * GROUP, (g + 1) * GROUP),
                slice(g * stacked, (g + 1) * stacked),
            )

        def score(i, g):
            at, cols, _ = places(i, g)
            return dot_t(keys[at, cols], queries[g])

        pooled = [[] for _ in range(images)]
        inverse = [[] for _ in range(images)]
        ahead = score(*units[0])
        for n, (i, g) in enumerate(units):
            at, cols, to = places(i, g)
            scores = ahead
            if n + 1 < len(units):
                ahead = score(*units[n + 1])
            if n < len(before):
                before[n]()
            rows_ = []
            weights = []
            for part_ in by_head(scores, block):
                part_ = jnp.exp(part_ - jnp.max(part_, axis=0, keepdims=True))
                rows_.append(1.0 / jnp.sum(part_, axis=0, keepdims=True))
                weights.append(part_.astype(BF16))
            inverse[i].append(jnp.concatenate(rows_, axis=1))
            weights = jnp.concatenate(weights, axis=1)
            weights_ref[which, at, to] = weights
            pooled[i].append(head_blocks(dot(values_t[cols, at], weights) * inverse[i][g], block))
        pooled_t = pooled
        pooled = [jnp.concatenate(found, axis=0).T.astype(BF16) for found in pooled]
        mixed = dot(jnp.concatenate(pooled, axis=0), wo[...])
        caption_2 = jnp.concatenate([caption] * images, axis=0)
        owner_2 = jnp.concatenate([owner] * images, axis=0)
        image = (
            lax.broadcasted_iota(jnp.int32, (images * block, 1), 0) // block + me * images
        ).astype(F32)
        inner = jnp.sum(mixed * caption_2, axis=1, keepdims=True)
        mixed_inv = lax.rsqrt(jnp.sum(mixed * mixed, axis=1, keepdims=True) + NORM_EPS)
        caption_inv = lax.rsqrt(jnp.sum(caption * caption, axis=1, keepdims=True) + NORM_EPS)
        caption_inv = jnp.concatenate([caption_inv] * images, axis=0)
        cosine = inner * mixed_inv * caption_inv
        logit = LOGIT_SCALE * cosine + LOGIT_BIAS
        label = jnp.where(owner_2 == image, 1.0, -1.0)
        slope = -LOGIT_SCALE * label / (1.0 + jnp.exp(label * logit))
        across = slope * mixed_inv * caption_inv
        grad_mixed = across * caption_2 - (slope * cosine * mixed_inv * mixed_inv) * mixed
        grad_pooled_t = dot_t(wo[...], grad_mixed.astype(BF16))
        if own:
            direct = across * mixed - (slope * cosine * caption_inv * caption_inv) * caption_2
            direct = sum(direct[i * block : (i + 1) * block] for i in range(images))

        grad_pooled = []
        means = []
        for i in range(images):
            scale = jnp.concatenate(
                [
                    jnp.broadcast_to(row, (HEAD_DIM, block))
                    for rows_ in inverse[i]
                    for row in by_head(rows_, block)
                ],
                axis=0,
            )
            found = (grad_pooled_t[:, i * block : (i + 1) * block] * scale).astype(BF16)
            grad_pooled.append(found.T)
            products = found.astype(F32) * jnp.concatenate(pooled_t[i], axis=0)
            products = [
                jnp.sum(products[h * HEAD_DIM : (h + 1) * HEAD_DIM], axis=0, keepdims=True)
                for h in range(d // HEAD_DIM)
            ]
            means.append(
                [
                    jnp.concatenate(
                        products[g * HEADS_IN_GROUP : (g + 1) * HEADS_IN_GROUP], axis=1
                    )
                    for g in range(groups)
                ]
            )

        def grad_weight(i, g):
            at, cols, _ = places(i, g)
            grads = head_stack(grad_pooled[i][:, cols])
            return grads, dot_t(values[at, cols], grads)

        grad_query = [None] * groups
        ahead = grad_weight(*units[0])
        for n, (i, g) in enumerate(units):
            at, cols, to = places(i, g)
            grads, grad_weights = ahead
            if n + 1 < len(units):
                ahead = grad_weight(*units[n + 1])
            weights = weights_ref[which, at, to].astype(F32)
            grad_scores = (weights * (grad_weights - means[i][g])).astype(BF16)
            later.append(
                functools.partial(finish, at, cols, to, grads, grad_scores, queries[g], which)
            )
            if own:
                found = head_blocks(dot(keys_t[cols, at], grad_scores), block)
                grad_query[g] = found if grad_query[g] is None else grad_query[g] + found
            else:
                later.pop()()
                if blocks == 1 and which == ns - 1 and g == groups - 1:
                    token_product(at)
        if own:
            grad_query = jnp.concatenate(grad_query, axis=0).T * HEAD_DIM**-0.5
            grad = direct + dot_t(grad_query.astype(BF16), wq[...])
            grad = grad.reshape(slots, rows, d)
            part[pl.ds(slot, slots)] = jnp.concatenate(
                [grad[:, :, :half], grad[:, :, half:]], axis=1
            ).astype(BF16)
        return later

    def token_product(at):
        token_out[at, :] = patches * (dot_t(gk_b[at, :], wk[...]) + dot_t(gv_b[at, :], wv[...]))

    def finish(at, cols, to, grads, grad_scores, queries, which):
        add(gv, gv_b, at, cols, dot(weights_ref[which, at, to], grads), which)
        add(gk, gk_b, at, cols, dot(grad_scores, queries), which)

    def run_all(which, own, before=()):
        if blocks == 1:
            return run_block(0, which, own, before)

        @pl.loop(0, blocks)
        def _(n):
            for work in run_block(n * slots, which, own):
                work()

        return []

    later = run_all(0, True)

    @pl.loop(1, nb, unroll=unroll)
    def _(step):
        part_copy(step).start()

    for step in range(1, ns):
        span_copy(step, step).wait_recv()
        span_owner_copy(step, step).wait_recv()
        later = run_all(step, False, later)
    for work in later:
        work()
    if blocks > 1:
        gk_b[...] = gk[...].astype(BF16)
        gv_b[...] = gv[...].astype(BF16)
    if blocks > 1 or ns == 1:
        for i in range(images):
            token_product(slice(i * patches, (i + 1) * patches))

    all_parts.wait_recv()

    parts_in[me] = part[me]
    sum_out[...] = jnp.sum(parts_in[...].astype(F32), axis=0)

    all_caps.wait_send()
    all_owners.wait_send()
    all_parts.wait_send()

    for step in range(1, ns):
        span_copy(step, ns - step).wait_send()
        span_owner_copy(step, ns - step).wait_send()


def write_kernel(sum_ref, token_ref, caption_out, token_out, unfolded, sems):
    rows, d = caption_out.shape
    count = sems.shape[0] - 1
    chunk = token_ref.shape[0] // count
    copies = [
        pltpu.make_async_copy(
            token_ref.at[pl.ds(n * chunk, chunk)],
            token_out.at[pl.ds(n * chunk, chunk)],
            sems.at[n],
        )
        for n in range(count)
    ]
    for copy in copies:
        copy.start()
    summed = sum_ref[...] * CAPTION_SCALE
    unfolded[...] = jnp.concatenate([summed[:rows], summed[rows:]], axis=1)
    copies.append(pltpu.make_async_copy(unfolded, caption_out, sems.at[count]))
    copies[-1].start()
    for copy in copies:
        copy.wait()


def hold(x):
    return pltpu.with_memory_space_constraint(x, pltpu.HBM)


def on_device(nb, ns, image_tokens, captions, owner, w_query, w_key, w_value, w_out):
    images, patches, d = image_tokens.shape
    rows = captions.shape[0]
    total = images * patches
    block = math.gcd(nb * rows, LANES)
    vmem = pl.BlockSpec(memory_space=pltpu.VMEM)
    hbm = pl.BlockSpec(memory_space=pltpu.HBM)
    heads = d // HEAD_DIM
    dma = pltpu.SemaphoreType.DMA
    token_terms, summed = pl.pallas_call(
        functools.partial(pair_kernel, nb, ns, images),
        out_shape=(
            jax.ShapeDtypeStruct((total, d), F32),
            jax.ShapeDtypeStruct((2 * rows, d // 2), F32),
        ),
        in_specs=[hbm] * 7,
        out_specs=(vmem, vmem),
        scratch_shapes=[
            pltpu.VMEM((rows, d), BF16),
            pltpu.VMEM((1, rows), jnp.int32),
            pltpu.VMEM((total, d), BF16),
            pltpu.VMEM((d, d), BF16),
            pltpu.VMEM((d, d), BF16),
            pltpu.VMEM((d, d), BF16),
            pltpu.VMEM((d, d), BF16),
            pltpu.VMEM((total, d), BF16),
            pltpu.VMEM((total, d), BF16),
            pltpu.VMEM((d, total), BF16),
            pltpu.VMEM((d, total), BF16),
            pltpu.VMEM((ns, total, heads * block), BF16),
            pltpu.VMEM((total, d), F32),
            pltpu.VMEM((total, d), F32),
            pltpu.VMEM((total, d), BF16),
            pltpu.VMEM((total, d), BF16),
            pltpu.VMEM((ns, nb, 2 * rows, d // 2), BF16),
            pltpu.VMEM((ns, nb, 1, LANES), jnp.int32),
            pltpu.VMEM((nb, 2 * rows, d // 2), BF16),
            pltpu.VMEM((nb, 2 * rows, d // 2), BF16),
            dma((7,)),
            dma,
            dma,
            dma,
            dma,
            dma((ns,)),
            dma((ns,)),
            dma((ns,)),
            dma((ns,)),
            dma,
            dma,
        ],
        compiler_params=pltpu.CompilerParams(
            collective_id=0, has_side_effects=True, vmem_limit_bytes=36 * 2**20
        ),
        name="pairs",
    )(
        hold(captions),
        hold(owner.reshape(1, rows)),
        hold(image_tokens.reshape(total, d)),
        hold(w_query),
        hold(w_key),
        hold(w_value),
        hold(w_out),
    )
    caption_grad, token_grad = pl.pallas_call(
        write_kernel,
        out_shape=(
            jax.ShapeDtypeStruct((rows, d), F32),
            jax.ShapeDtypeStruct((total, d), F32),
        ),
        in_specs=[vmem, vmem],
        out_specs=(hbm, hbm),
        scratch_shapes=[
            pltpu.VMEM((rows, d), F32),
            dma((2 * images + 1,)),
        ],
        compiler_params=pltpu.CompilerParams(vmem_limit_bytes=16 * 2**20),
        name="write",
    )(summed, token_terms)
    return (caption_grad, token_grad.reshape(images, patches, d))


def solution(mesh):
    placed = (
        P("batch", None, None),
        P(("batch", "span"), None),
        P(("batch", "span")),
        P(),
        P(),
        P(),
        P(),
    )
    return jax.shard_map(
        functools.partial(on_device, mesh.shape["batch"], mesh.shape["span"]),
        mesh=mesh,
        in_specs=placed,
        out_specs=(P(("batch", "span"), None), P("batch", None, None)),
        check_vma=False,
    )
```
